512 devices in a mesh: ctx: 32 (over y_hi, z, core), tp: 16 (over y_lo, x).
Axes of the slice: x: 4, y: 8 (y_hi: 2, y_lo: 4; y = y_hi * 4 + y_lo), z: 8, core: 2. Of those that a mesh axis runs over, the one named last changes fastest.
Arguments:
- queries: bfloat16 [4096, 8192], P('ctx', 'tp'), may hold values from -6 to 6
- keys_in: bfloat16 [4096, 8192], P('ctx', 'tp'), may hold values from -6 to 6
- values_in: bfloat16 [4096, 8192], P('ctx', 'tp'), may hold values from -6 to 6
- decay_rates: float32 [8192, 16], P('tp'), may hold values from 7.324219e-05 to 0.03
- residues: float32 [8192, 16], P('tp'), may hold values from -1.5 to 1.5
- skip_gain: float32 [8192], P('tp'), may hold values from -4 to 4
- cotangent: bfloat16 [4096, 8192], P('ctx', 'tp'), may hold values from -6 to 6
Outputs:
- operator_out: bfloat16 [4096, 8192], P('ctx', 'tp')
- grad_queries: bfloat16 [4096, 8192], P('ctx', 'tp')
- grad_keys: bfloat16 [4096, 8192], P('ctx', 'tp')
- grad_values: bfloat16 [4096, 8192], P('ctx', 'tp')
- grad_residues: float32 [8192, 16], P('tp')
The draws below stay inside these ranges and needn't reach their ends.
All inputs are finite; a program needn't handle non-finite values.
Results may differ from the reference program's by a relative error of at most 0.0054.
Values may be sent and summed in bfloat16 or wider, within the bound.
A program may use at most 64 MiB of HBM per device.

```python
import math
import jax
import jax.numpy as jnp
from jax import lax

D = 8192
ORDER = 16
SEQ = 4096


def level_of(key, dims, split, low, high):
    loudness, own = 1.0, jax.random.fold_in(key, 6)
    for axis_at, blocks in split:
        heights = jnp.exp(jax.random.uniform(jax.random.fold_in(own, axis_at), (blocks,), jnp.float32, low / len(split), high / len(split)))
        loudness = loudness * jnp.repeat(heights, dims[axis_at] // blocks).reshape([-1 if axis == axis_at else 1 for axis in range(len(dims))])
    return loudness


def bell_draw(rng, dims, deviation, limit, pieces=(), kind=jnp.bfloat16):
    result = jax.random.normal(rng, dims, jnp.float32) * deviation
    if len(pieces) > 0:
        result = level_of(rng, dims, pieces, -0.22, 0.18) * result
    return jnp.clip(result, min=-limit, max=limit).astype(kind)


def setup_inputs(seed: int = 0) -> dict:
    streams_of = jax.random.split(jax.random.key(seed), 8)
    queries = bell_draw(streams_of[0], (SEQ, D), 1.0, 6.0, ((0, 32), (1, 16)))
    keys_in = bell_draw(streams_of[1], (SEQ, D), 1.0, 6.0, ((0, 32), (1, 16)))
    values_in = bell_draw(streams_of[2], (SEQ, D), 1.0, 6.0, ((0, 32), (1, 16)))
    decay_rates = jnp.clip(jnp.exp(math.log(0.03) - 6.015181 * jax.random.uniform(streams_of[3], (D, ORDER), jnp.float32) ** level_of(streams_of[3], (D, ORDER), ((0, 16),), -0.2, 0.2)), 7.324219041038305e-05, 0.03)
    residues = bell_draw(streams_of[4], (D, ORDER), 0.25, 1.5, ((0, 16),), jnp.float32)
    skip_gain = bell_draw(streams_of[5], (D,), 1.0, 4.0, ((0, 16),), jnp.float32)
    cotangent = bell_draw(streams_of[6], (SEQ, D), 1.0, 6.0, ((0, 32), (1, 16)))
    return dict(queries=queries, keys_in=keys_in, values_in=values_in, decay_rates=decay_rates, residues=residues, skip_gain=skip_gain, cotangent=cotangent)


PRECISE = lax.Precision.HIGHEST

def causal_conv(signal, taps, length):
    padded_len = 2 * length
    spectrum = jnp.fft.rfft(signal, n=padded_len, axis=0) * jnp.fft.rfft(taps, n=padded_len, axis=0)
    return jnp.fft.irfft(spectrum, n=padded_len, axis=0)[:length]

def lagged_sums(later_sig, earlier_sig, length):
    padded_len = 2 * length
    spectrum = jnp.fft.rfft(later_sig, n=padded_len, axis=0) * jnp.conj(jnp.fft.rfft(earlier_sig, n=padded_len, axis=0))
    return jnp.fft.irfft(spectrum, n=padded_len, axis=0)[:length]

def reference(queries, keys_in, values_in, decay_rates, residues, skip_gain, cotangent):
    length = queries.shape[0]
    channels = queries.shape[1]
    queries_f = queries.astype(jnp.float32)
    keys_f = keys_in.astype(jnp.float32)
    values_f = values_in.astype(jnp.float32)
    cot_f = cotangent.astype(jnp.float32)
    gated = lax.optimization_barrier((keys_f * values_f).astype(jnp.bfloat16))
    pulled = lax.optimization_barrier((cot_f * queries_f).astype(jnp.bfloat16))
    positions = jnp.arange(length, dtype=jnp.float32)
    group_width = min(channels, 128)
    group_count = channels // group_width

    def one_group(group_index):
        start = group_index * group_width
        gated_block = lax.dynamic_slice_in_dim(gated, start, group_width, 1).astype(jnp.float32)
        pulled_block = lax.dynamic_slice_in_dim(pulled, start, group_width, 1).astype(jnp.float32)
        rate_block = lax.dynamic_slice_in_dim(decay_rates, start, group_width, 0)
        residue_block = lax.dynamic_slice_in_dim(residues, start, group_width, 0)
        powers = jnp.exp(-rate_block[None] * positions[:, None, None])
        unit_scale = jnp.sqrt(1.0 - jnp.exp(-2.0 * rate_block))
        mode_coef = residue_block * unit_scale
        filter_taps = jnp.einsum('tcn,cn->tc', powers, mode_coef, precision=PRECISE)
        convolved = causal_conv(gated_block, filter_taps, length)
        adjoint = causal_conv(pulled_block[::-1], filter_taps, length)[::-1]
        lags = lagged_sums(pulled_block, gated_block, length)
        raw_grad = unit_scale * jnp.einsum('tc,tcn->cn', lags, powers, precision=PRECISE)
        return (convolved, adjoint, raw_grad)
    convolved, adjoint, raw_grad = lax.map(one_group, jnp.arange(group_count, dtype=jnp.int32))
    convolved = jnp.moveaxis(convolved, 0, 1).reshape(length, channels)
    adjoint = jnp.moveaxis(adjoint, 0, 1).reshape(length, channels)
    raw_grad = raw_grad.reshape(channels, decay_rates.shape[1])
    convolved = lax.optimization_barrier(convolved.astype(jnp.bfloat16))
    adjoint = lax.optimization_barrier(adjoint.astype(jnp.bfloat16))
    mixed = convolved.astype(jnp.float32) + skip_gain[None, :] * gated.astype(jnp.float32)
    operator_out = (queries_f * mixed).astype(jnp.bfloat16)
    grad_queries = (cot_f * mixed).astype(jnp.bfloat16)
    grad_gated = adjoint.astype(jnp.float32) + skip_gain[None, :] * pulled.astype(jnp.float32)
    grad_keys = (grad_gated * values_f).astype(jnp.bfloat16)
    grad_values = (grad_gated * keys_f).astype(jnp.bfloat16)
    grad_square = jnp.sum(raw_grad * raw_grad)
    factor = jnp.minimum(1.0, math.sqrt(D * ORDER) / jnp.sqrt(grad_square + 1e-06))
    grad_residues = raw_grad * factor
    return (operator_out, grad_queries, grad_keys, grad_values, grad_residues)
```

```python
import math

import jax
import jax.numpy as jnp
from jax import lax
from jax.experimental import pallas as pl
from jax.experimental.pallas import tpu as pltpu
from jax.sharding import PartitionSpec as P

D = 8192
ORDER = 16
LANES = 128
ROWS = 8
SEG = 16
NSEG = 8
CTX = 32
MESH = pl.DeviceIdType.MESH


def kernel(
    q_hbm, k_hbm, v_hbm, c_hbm, dec_hbm, res_hbm, skip_hbm,
    op_hbm, gq_hbm, gk_hbm, gv_hbm, gr_hbm,
    q_in, k_in, v_in, c_in, dec, res, skip,
    op_out, gq_out, gk_out, gv_out, gr_out,
    xs, ps, hs, gs, far, pw, taps, yl, zl, yn, zn, dt,
    send1, recv1, send2, recv2, part,
    in_sems, out_sems, send_sems, recv_sems,
):
    me, mt = lax.axis_index("ctx"), lax.axis_index("tp")
    n_tp = part.shape[0]
    rows, chans = q_in.shape
    cts = chans // LANES

    ins = [
        pltpu.make_async_copy(src, dst, in_sems.at[i])
        for i, (src, dst) in enumerate(
            zip((dec_hbm, res_hbm, skip_hbm, k_hbm, v_hbm, q_hbm, c_hbm), (dec, res, skip, k_in, v_in, q_in, c_in))
        )
    ]
    for copy in ins[3:] + ins[:3]:
        copy.start()

    barrier = pltpu.get_barrier_semaphore()

    @pl.loop(1, CTX)
    def _(off):
        pl.semaphore_signal(barrier, inc=1, device_id={"ctx": lax.rem(me + off, CTX)}, device_id_type=MESH)

    @pl.loop(1, n_tp)
    def _(off):
        pl.semaphore_signal(barrier, inc=1, device_id={"tp": lax.rem(mt + off, n_tp)}, device_id_type=MESH)

    def lanes(ct):
        return pl.ds(ct * LANES, LANES)

    for copy in ins:
        copy.wait()

    for ct in range(cts):
        for r in range(rows // 16):
            at = (pl.ds(r * 16, 16), lanes(ct))
            to = pl.ds(ct * rows + r * 16, 16)
            kv = k_in[at].astype(jnp.float32) * v_in[at].astype(jnp.float32)
            cq = c_in[at].astype(jnp.float32) * q_in[at].astype(jnp.float32)
            xs[to, :] = kv.astype(jnp.bfloat16).astype(jnp.float32)
            ps[to, :] = cq.astype(jnp.bfloat16).astype(jnp.float32)

    pieces = [(half, ct) for half in range(2) for ct in range(cts)]
    rate = [dec[pl.ds(half * ROWS, ROWS), lanes(ct)] for half, ct in pieces]
    decay = [jnp.exp(-d) for d in rate]

    for (half, ct), d in zip(pieces, rate):
        for pair in range(4):
            dt[pl.ds(ct * 64 + 2 * pair + half, ROWS, stride=ROWS), :] = d

    def wide(ref, row):
        return jnp.broadcast_to(ref[pl.ds(row, 1), :], (ROWS, LANES))

    zeros = [jnp.zeros((ROWS, LANES), jnp.float32) for _ in pieces]

    def scan_segment(r, state):
        fwd, inner, bwd = (list(part_) for part_ in state)
        back = NSEG - 1 - r
        for j, (half, ct) in enumerate(pieces):
            hs[pl.ds(pl.multiple_of(ct * rows + r * SEG + half * ROWS, ROWS), ROWS), :] = fwd[j]
            gs[pl.ds(pl.multiple_of(ct * rows + back * SEG + half * ROWS, ROWS), ROWS), :] = bwd[j]
        for i in range(SEG):
            for ct in range(cts):
                x = wide(xs, ct * rows + r * SEG + i)
                p = wide(ps, ct * rows + r * SEG + i)
                pb = wide(ps, ct * rows + back * SEG + (SEG - 1 - i))
                for half in range(2):
                    j = half * cts + ct
                    fwd[j] = fwd[j] * decay[j] + x
                    inner[j] = inner[j] + fwd[j] * p
                    bwd[j] = bwd[j] * decay[j] + pb
        return fwd, inner, bwd

    fwd, inner, bwd = lax.fori_loop(0, NSEG, scan_segment, (zeros, zeros, zeros))

    for j, (half, ct) in enumerate(pieces):
        for pair, value in enumerate((fwd[j], bwd[j], inner[j], zeros[j])):
            send1[pl.ds(ct * 64 + 2 * pair + half, ROWS, stride=ROWS), :] = value

    def tile(index):
        return pl.ds(pl.multiple_of(index * ROWS, ROWS), ROWS)

    pl.semaphore_wait(barrier, CTX - 1 + n_tp - 1)

    def exchange(src, dst, which):
        @pl.loop(1, CTX)
        def _(off):
            to = lax.rem(me + off, CTX)
            pltpu.make_async_remote_copy(
                src_ref=src.at[tile(to), :],
                dst_ref=dst.at[tile(me), :],
                send_sem=send_sems.at[which],
                recv_sem=recv_sems.at[which],
                device_id={"ctx": to},
                device_id_type=MESH,
            ).start()

    def arrived(dst, sem):
        most = dst.at[pl.ds(0, (CTX - 1) * ROWS), :]
        pltpu.make_async_copy(most, most, sem).wait()

    exchange(send1, recv1, 0)
    recv1[tile(me), :] = send1[tile(me), :]

    unit = [jnp.sqrt(1.0 - jnp.exp(-2.0 * d)) for d in rate]
    coef = [
        res[pl.ds(half * ROWS, ROWS), lanes(ct)] * unit[j] for j, (half, ct) in enumerate(pieces)
    ]

    @pl.loop(0, SEG + 1)
    def _(i):
        lag = i.astype(jnp.float32)
        for ct in range(cts):
            total = None
            for half in range(2):
                j = half * cts + ct
                power = coef[j] * jnp.exp(-rate[j] * lag)
                pw[pl.ds(pl.multiple_of((ct * (SEG + 1) + i) * ORDER + half * ROWS, ROWS), ROWS), :] = power
                total = power if total is None else total + power
            total = jnp.sum(total, axis=0, keepdims=True)
            taps[tile(ct * (SEG + 1) + i), :] = jnp.broadcast_to(total, (ROWS, LANES))

    @pl.loop(0, NSEG)
    def _(r):
        lag = (r * SEG).astype(jnp.float32)
        for j, (half, ct) in enumerate(pieces):
            far[pl.ds(pl.multiple_of(ct * rows + r * SEG + half * ROWS, ROWS), ROWS), :] = jnp.exp(-rate[j] * lag)

    @pl.loop(0, cts)
    def _(ct):
        x = [xs[pl.ds(ct * rows + i, NSEG, stride=SEG), :] for i in range(SEG)]
        p = [ps[pl.ds(ct * rows + i, NSEG, stride=SEG), :] for i in range(SEG)]
        tap = [taps[tile(ct * (SEG + 1) + i), :] for i in range(SEG)]
        for i in range(SEG):
            y = x[i] * tap[0]
            for lag in range(1, i + 1):
                y = y + x[i - lag] * tap[lag]
            yl[tile(ct * SEG + i), :] = y
            z = p[i] * tap[0]
            for lag in range(1, SEG - i):
                z = z + p[i + lag] * tap[lag]
            zl[tile(ct * SEG + i), :] = z

    mine = dt[tile(me), :]
    block = jnp.exp(-float(rows) * mine)
    step = jnp.exp(-mine)
    line = lax.broadcasted_iota(jnp.int32, (ROWS, LANES), 0)
    zero = jnp.zeros((ROWS, LANES), jnp.float32)
    arrived(recv1, recv_sems.at[0])

    carry, cross, inside = zero, zero, zero
    for e in range(CTX):
        got = recv1[pl.ds(e * ROWS, ROWS), :]
        send2[pl.ds(e * ROWS, ROWS), :] = carry
        cross = cross + pltpu.roll(got, ROWS - 2, 0) * carry
        inside = inside + got
        carry = carry * block + got
    raw_tile = inside + pltpu.roll(step * cross, 4, 0)
    carry = zero
    for e in reversed(range(CTX)):
        got = recv1[pl.ds(e * ROWS, ROWS), :]
        before = send2[pl.ds(e * ROWS, ROWS), :]
        send2[pl.ds(e * ROWS, ROWS), :] = jnp.where(line < 2, before, jnp.where(line < 4, carry, raw_tile))
        carry = carry * block + got

    exchange(send2, recv2, 1)
    recv2[tile(me), :] = send2[tile(me), :]
    arrived(recv2, recv_sems.at[1])

    def from_owners(pair, half, ct):
        return recv2[pl.ds(ct * 64 + 2 * pair + half, ROWS, stride=ROWS), :]

    raw = [unit[j] * from_owners(2, half, ct) for j, (half, ct) in enumerate(pieces)]
    square = raw[0] * raw[0]
    for value in raw[1:]:
        square = square + value * value
    part[mt] = jnp.sum(square, axis=0, keepdims=True)

    @pl.loop(1, n_tp)
    def _(off):
        pltpu.make_async_remote_copy(
            src_ref=part.at[mt],
            dst_ref=part.at[mt],
            send_sem=send_sems.at[2],
            recv_sem=recv_sems.at[2],
            device_id={"tp": lax.rem(mt + off, n_tp)},
            device_id_type=MESH,
        ).start()

    before = [from_owners(0, half, ct) for half, ct in pieces]
    after = [from_owners(1, half, ct) for half, ct in pieces]

    @pl.loop(0, NSEG)
    def _(r):
        for j, (half, ct) in enumerate(pieces):
            here = pl.ds(pl.multiple_of(ct * rows + r * SEG + half * ROWS, ROWS), ROWS)
            there = pl.ds(pl.multiple_of(ct * rows + (NSEG - 1 - r) * SEG + half * ROWS, ROWS), ROWS)
            hs[here, :] = hs[here, :] + far[here, :] * before[j]
            gs[here, :] = gs[here, :] + far[there, :] * after[j]

    def out_copies(at):
        return [
            pltpu.make_async_copy(src.at[at], dst.at[at], out_sems.at[i])
            for i, (src, dst) in enumerate(
                ((op_out, op_hbm), (gq_out, gq_hbm), (gk_out, gk_hbm), (gv_out, gv_hbm))
            )
        ]

    @pl.loop(0, cts)
    def _(ct):
        h = [hs[pl.ds(ct * rows + n, NSEG, stride=SEG), :] for n in range(ORDER)]
        g = [gs[pl.ds(ct * rows + n, NSEG, stride=SEG), :] for n in range(ORDER)]
        for i in range(SEG):
            y = yl[tile(ct * SEG + i), :]
            z = zl[tile(ct * SEG + SEG - 1 - i), :]
            ys, zs = [], []
            for n in range(ORDER):
                power = wide(pw, (ct * (SEG + 1) + i + 1) * ORDER + n)
                ys.append(power * h[n])
                zs.append(power * g[n])
            while len(ys) > 1:
                ys = [a + b for a, b in zip(ys[::2], ys[1::2])]
                zs = [a + b for a, b in zip(zs[::2], zs[1::2])]
            yn[pl.ds(ct * rows + i, NSEG, stride=SEG), :] = y + ys[0]
            zn[pl.ds(ct * rows + SEG - 1 - i, NSEG, stride=SEG), :] = z + zs[0]
        cols = pl.ds(pl.multiple_of(ct * LANES, LANES), LANES)
        gain = jnp.broadcast_to(skip[:, cols], (SEG, LANES))
        for r in range(rows // SEG):
            at = (pl.ds(r * SEG, SEG), cols)
            here = pl.ds(pl.multiple_of(ct * rows + r * SEG, SEG), SEG)
            conv = yn[here, :].astype(jnp.bfloat16).astype(jnp.float32)
            adj = zn[here, :].astype(jnp.bfloat16).astype(jnp.float32)
            mixed = conv + gain * xs[here, :]
            grad = adj + gain * ps[here, :]
            op_out[at] = (q_in[at].astype(jnp.float32) * mixed).astype(jnp.bfloat16)
            gq_out[at] = (c_in[at].astype(jnp.float32) * mixed).astype(jnp.bfloat16)
            gk_out[at] = (v_in[at].astype(jnp.float32) * grad).astype(jnp.bfloat16)
            gv_out[at] = (k_in[at].astype(jnp.float32) * grad).astype(jnp.bfloat16)
        for copy in out_copies((slice(None), cols)):
            copy.start()

    others = part.at[pl.ds(0, n_tp - 1)]
    pltpu.make_async_copy(others, others, recv_sems.at[2]).wait()
    total = jnp.sum(jnp.sum(part[...], axis=0), axis=1, keepdims=True)
    factor = jnp.minimum(1.0, math.sqrt(D * ORDER) / jnp.sqrt(total + 1e-06))
    for j, (half, ct) in enumerate(pieces):
        gr_out[pl.ds(half * ROWS, ROWS), lanes(ct)] = raw[j] * factor
    last = pltpu.make_async_copy(gr_out, gr_hbm, out_sems.at[4])
    last.start()
    arrived(send1, send_sems.at[0])
    arrived(send2, send_sems.at[1])
    pltpu.make_async_copy(others, others, send_sems.at[2]).wait()
    for copy in out_copies((slice(None), slice(None))):
        copy.wait()
    last.wait()


def shards(queries, keys_in, values_in, decay_rates, residues, skip_gain, cotangent):
    rows, chans = queries.shape
    n_tp = lax.axis_size("tp")
    cts = chans // LANES
    f32, bf16 = jnp.float32, jnp.bfloat16
    line = jax.ShapeDtypeStruct((rows, chans), bf16)
    anywhere = pl.BlockSpec(memory_space=pl.ANY)
    table = pltpu.VMEM((cts * rows, LANES), f32)
    posts = pltpu.VMEM((CTX * ROWS, LANES), f32)
    outs = pl.pallas_call(
        kernel,
        out_shape=(line, line, line, line, jax.ShapeDtypeStruct((ORDER, chans), f32)),
        in_specs=[anywhere] * 7,
        out_specs=(anywhere,) * 5,
        scratch_shapes=[
            *[pltpu.VMEM((rows, chans), bf16)] * 4,
            pltpu.VMEM((ORDER, chans), f32),
            pltpu.VMEM((ORDER, chans), f32),
            pltpu.VMEM((1, chans), f32),
            *[pltpu.VMEM((rows, chans), bf16)] * 4,
            pltpu.VMEM((ORDER, chans), f32),
            *[table] * 5,
            pltpu.VMEM((cts * (SEG + 1) * ORDER, LANES), f32),
            pltpu.VMEM((cts * (SEG + 1) * ROWS, LANES), f32),
            *[table] * 4,
            posts,
            *[posts] * 4,
            pltpu.VMEM((n_tp, 1, LANES), f32),
            pltpu.SemaphoreType.DMA((7,)),
            pltpu.SemaphoreType.DMA((5,)),
            pltpu.SemaphoreType.DMA((3,)),
            pltpu.SemaphoreType.DMA((3,)),
        ],
        compiler_params=pltpu.CompilerParams(collective_id=0, has_side_effects=True, vmem_limit_bytes=32 * 2**20),
        name="modal_conv",
    )(queries, keys_in, values_in, cotangent, decay_rates.T, residues.T, skip_gain.reshape(1, chans))
    return (*outs[:4], outs[4].T)


def solution(mesh):
    line, modes = P("ctx", "tp"), P("tp", None)
    in_specs = (line, line, line, modes, modes, P("tp"), line)
    out_specs = (line, line, line, line, modes)
    return jax.shard_map(shards, mesh=mesh, in_specs=in_specs, out_specs=out_specs, check_vma=False)
```

```python
import math

import jax
import jax.numpy as jnp
from jax import lax
from jax.experimental import pallas as pl
from jax.experimental.pallas import tpu as pltpu
from jax.sharding import PartitionSpec as P

D = 8192
ORDER = 16
LANES = 128
ROWS = 8
SEG = 16
NSEG = 8
CTX = 32
OWNERS = 16
PIECES = 2
MESH = pl.DeviceIdType.MESH


def kernel(
    q_hbm, k_hbm, v_hbm, c_hbm, dec_hbm, res_hbm, skip_hbm,
    op_hbm, gq_hbm, gk_hbm, gv_hbm, gr_hbm,
    q_in, k_in, v_in, c_in, dec, res, skip,
    op_out, gq_out, gk_out, gv_out, gr_out,
    xs, ps, hs, gs, far, pw, taps, yl, zl, yn, zn,
    send1, recv1, send2, recv2, plane, column,
    in_sems, out_sems, send_sems, recv_sems,
):
    me, mt = lax.axis_index("ctx"), lax.axis_index("tp")
    n_tp = plane.shape[0] // 2
    upper, line = me // (CTX // 2), lax.rem(me, CTX // 2)
    early = line < OWNERS // 2
    there = lax.rem(mt + n_tp // 2, n_tp)
    slot = upper * (OWNERS // 2) + line
    spot = upper * n_tp + mt
    rows, chans = q_in.shape
    cts = chans // LANES

    ins = [
        pltpu.make_async_copy(src, dst, in_sems.at[i])
        for i, (src, dst) in enumerate(
            zip((dec_hbm, res_hbm, skip_hbm, k_hbm, v_hbm, q_hbm, c_hbm), (dec, res, skip, k_in, v_in, q_in, c_in))
        )
    ]
    for copy in ins[3:] + ins[:3]:
        copy.start()

    barrier = pltpu.get_barrier_semaphore()

    def in_plane(off):
        other = lax.rem(spot + off, 2 * n_tp)
        return {"ctx": other // n_tp * (CTX // 2) + line, "tp": lax.rem(other, n_tp)}

    @pl.when(early)
    def _():
        @pl.loop(0, CTX)
        def _(off):
            to = {"ctx": lax.rem(me + off, CTX), "tp": there}
            pl.semaphore_signal(barrier, inc=1, device_id=to, device_id_type=MESH)

        @pl.loop(1, 2 * n_tp)
        def _(off):
            pl.semaphore_signal(barrier, inc=1, device_id=in_plane(off), device_id_type=MESH)

    def lanes(ct):
        return pl.ds(ct * LANES, LANES)

    for copy in ins:
        copy.wait()

    for ct in range(cts):
        for r in range(rows // 16):
            at = (pl.ds(r * 16, 16), lanes(ct))
            to = pl.ds(ct * rows + r * 16, 16)
            kv = k_in[at].astype(jnp.float32) * v_in[at].astype(jnp.float32)
            cq = c_in[at].astype(jnp.float32) * q_in[at].astype(jnp.float32)
            xs[to, :] = kv.astype(jnp.bfloat16).astype(jnp.float32)
            ps[to, :] = cq.astype(jnp.bfloat16).astype(jnp.float32)

    pieces = [(half, ct) for half in range(2) for ct in range(cts)]
    rate = [dec[pl.ds(half * ROWS, ROWS), lanes(ct)] for half, ct in pieces]
    decay = [jnp.exp(-d) for d in rate]

    def wide(ref, row):
        return jnp.broadcast_to(ref[pl.ds(row, 1), :], (ROWS, LANES))

    zeros = [jnp.zeros((ROWS, LANES), jnp.float32) for _ in pieces]

    def scan_segment(r, state):
        fwd, inner, bwd = (list(part_) for part_ in state)
        back = NSEG - 1 - r
        for j, (half, ct) in enumerate(pieces):
            hs[pl.ds(pl.multiple_of(ct * rows + r * SEG + half * ROWS, ROWS), ROWS), :] = fwd[j]
            gs[pl.ds(pl.multiple_of(ct * rows + back * SEG + half * ROWS, ROWS), ROWS), :] = bwd[j]
        for i in range(SEG):
            for ct in range(cts):
                x = wide(xs, ct * rows + r * SEG + i)
                p = wide(ps, ct * rows + r * SEG + i)
                pb = wide(ps, ct * rows + back * SEG + (SEG - 1 - i))
                for half in range(2):
                    j = half * cts + ct
                    fwd[j] = fwd[j] * decay[j] + x
                    inner[j] = inner[j] + fwd[j] * p
                    bwd[j] = bwd[j] * decay[j] + pb
        return fwd, inner, bwd

    fwd, inner, bwd = lax.fori_loop(0, NSEG, scan_segment, (zeros, zeros, zeros))

    for j, (half, ct) in enumerate(pieces):
        for pair, value in enumerate((fwd[j], bwd[j], inner[j], rate[j])):
            send1[pl.ds(ct * 64 + 2 * pair + half, ROWS, stride=ROWS), :] = value

    def tile(index):
        return pl.ds(pl.multiple_of(index * ROWS, ROWS), ROWS)

    @pl.when(early)
    def _():
        pl.semaphore_wait(barrier, OWNERS + 2 * n_tp - 1)

    @pl.when(jnp.logical_not(early))
    def _():
        pl.semaphore_wait(barrier, OWNERS)

    def group(index):
        return pl.ds(pl.multiple_of(index * PIECES * ROWS, PIECES * ROWS), PIECES * ROWS)

    @pl.loop(0, OWNERS)
    def _(off):
        to = lax.rem(slot + off, OWNERS)
        pltpu.make_async_remote_copy(
            src_ref=send1.at[group(to), :],
            dst_ref=recv1.at[group(me), :],
            send_sem=send_sems.at[0],
            recv_sem=recv_sems.at[0],
            device_id={"ctx": to // (OWNERS // 2) * (CTX // 2) + lax.rem(to, OWNERS // 2), "tp": there},
            device_id_type=MESH,
        ).start()

    def wait_bytes(ref, sem):
        pltpu.make_async_copy(ref, ref, sem).wait()

    unit = [jnp.sqrt(1.0 - jnp.exp(-2.0 * d)) for d in rate]
    coef = [
        res[pl.ds(half * ROWS, ROWS), lanes(ct)] * unit[j] for j, (half, ct) in enumerate(pieces)
    ]

    @pl.loop(0, SEG + 1)
    def _(i):
        lag = i.astype(jnp.float32)
        for ct in range(cts):
            total = None
            for half in range(2):
                j = half * cts + ct
                power = coef[j] * jnp.exp(-rate[j] * lag)
                pw[pl.ds(pl.multiple_of((ct * (SEG + 1) + i) * ORDER + half * ROWS, ROWS), ROWS), :] = power
                total = power if total is None else total + power
            total = jnp.sum(total, axis=0, keepdims=True)
            taps[tile(ct * (SEG + 1) + i), :] = jnp.broadcast_to(total, (ROWS, LANES))

    @pl.loop(0, NSEG)
    def _(r):
        lag = (r * SEG).astype(jnp.float32)
        for j, (half, ct) in enumerate(pieces):
            far[pl.ds(pl.multiple_of(ct * rows + r * SEG + half * ROWS, ROWS), ROWS), :] = jnp.exp(-rate[j] * lag)

    @pl.loop(0, cts)
    def _(ct):
        x = [xs[pl.ds(ct * rows + i, NSEG, stride=SEG), :] for i in range(SEG)]
        p = [ps[pl.ds(ct * rows + i, NSEG, stride=SEG), :] for i in range(SEG)]
        tap = [taps[tile(ct * (SEG + 1) + i), :] for i in range(SEG)]
        for i in range(SEG):
            y = x[i] * tap[0]
            for lag in range(1, i + 1):
                y = y + x[i - lag] * tap[lag]
            yl[tile(ct * SEG + i), :] = y
            z = p[i] * tap[0]
            for lag in range(1, SEG - i):
                z = z + p[i + lag] * tap[lag]
            zl[tile(ct * SEG + i), :] = z

    row = lax.broadcasted_iota(jnp.int32, (ROWS, LANES), 0)

    @pl.when(early)
    def _():
        wait_bytes(recv1, recv_sems.at[0])

        def tiles(ref, e):
            return [ref[pl.ds((e * PIECES + i) * ROWS, ROWS), :] for i in range(PIECES)]

        def put(e, values):
            for i, value in enumerate(values):
                send2[pl.ds((e * PIECES + i) * ROWS, ROWS), :] = value

        rates = [
            jnp.where(
                row < 2,
                pltpu.roll(got, 2, 0),
                jnp.where(row < 4, pltpu.roll(got, 4, 0), jnp.where(row < 6, pltpu.roll(got, 6, 0), got)),
            )
            for got in tiles(recv1, 0)
        ]
        block = [jnp.exp(-float(rows) * r) for r in rates]
        zero = [jnp.zeros((ROWS, LANES), jnp.float32) for _ in rates]
        carry, cross, inside = list(zero), list(zero), list(zero)
        for e in range(CTX):
            put(e, carry)
            for i, got in enumerate(tiles(recv1, e)):
                cross[i] = cross[i] + pltpu.roll(got, 6, 0) * carry[i]
                inside[i] = inside[i] + got
                carry[i] = carry[i] * block[i] + got
        raw = [
            jnp.sqrt(1.0 - jnp.exp(-2.0 * r)) * (inside[i] + pltpu.roll(jnp.exp(-r) * cross[i], 4, 0))
            for i, r in enumerate(rates)
        ]
        carry = list(zero)
        for e in reversed(range(CTX)):
            before = tiles(send2, e)
            put(e, [jnp.where(row < 2, f, jnp.where(row < 4, b, g)) for f, b, g in zip(before, carry, raw)])
            for i, got in enumerate(tiles(recv1, e)):
                carry[i] = carry[i] * block[i] + got

        square = jnp.zeros((ROWS, LANES), jnp.float32)
        for value in raw:
            square = square + jnp.where((row >= 4) & (row < 6), value * value, 0.0)
        plane[spot] = jnp.sum(square, axis=0, keepdims=True)

        @pl.loop(1, 2 * n_tp)
        def _(off):
            pltpu.make_async_remote_copy(
                src_ref=plane.at[spot],
                dst_ref=plane.at[spot],
                send_sem=send_sems.at[2],
                recv_sem=recv_sems.at[2],
                device_id=in_plane(off),
                device_id_type=MESH,
            ).start()

        @pl.loop(0, CTX)
        def _(off):
            to = lax.rem(me + off, CTX)
            pltpu.make_async_remote_copy(
                src_ref=send2.at[group(to), :],
                dst_ref=recv2.at[group(slot), :],
                send_sem=send_sems.at[1],
                recv_sem=recv_sems.at[1],
                device_id={"ctx": to, "tp": there},
                device_id_type=MESH,
            ).start()

        wait_bytes(plane.at[pl.ds(0, 2 * n_tp - 1)], recv_sems.at[2])
        column[line] = jnp.sum(plane[...], axis=0)

        @pl.loop(1, CTX // 2)
        def _(off):
            pltpu.make_async_remote_copy(
                src_ref=column.at[line],
                dst_ref=column.at[line],
                send_sem=send_sems.at[3],
                recv_sem=recv_sems.at[3],
                device_id={"ctx": upper * (CTX // 2) + lax.rem(line + off, CTX // 2)},
                device_id_type=MESH,
            ).start()

    wait_bytes(recv2, recv_sems.at[1])

    def from_owners(pair, half, ct):
        return recv2[pl.ds(ct * 64 + 2 * pair + half, ROWS, stride=ROWS), :]

    before = [from_owners(0, half, ct) for half, ct in pieces]
    after = [from_owners(1, half, ct) for half, ct in pieces]

    @pl.loop(0, NSEG)
    def _(r):
        for j, (half, ct) in enumerate(pieces):
            here = pl.ds(pl.multiple_of(ct * rows + r * SEG + half * ROWS, ROWS), ROWS)
            mirror = pl.ds(pl.multiple_of(ct * rows + (NSEG - 1 - r) * SEG + half * ROWS, ROWS), ROWS)
            hs[here, :] = hs[here, :] + far[here, :] * before[j]
            gs[here, :] = gs[here, :] + far[mirror, :] * after[j]

    def out_copies(at):
        return [
            pltpu.make_async_copy(src.at[at], dst.at[at], out_sems.at[i])
            for i, (src, dst) in enumerate(
                ((op_out, op_hbm), (gq_out, gq_hbm), (gk_out, gk_hbm), (gv_out, gv_hbm))
            )
        ]

    @pl.loop(0, cts)
    def _(ct):
        h = [hs[pl.ds(ct * rows + n, NSEG, stride=SEG), :] for n in range(ORDER)]
        g = [gs[pl.ds(ct * rows + n, NSEG, stride=SEG), :] for n in range(ORDER)]
        for i in range(SEG):
            y = yl[tile(ct * SEG + i), :]
            z = zl[tile(ct * SEG + SEG - 1 - i), :]
            ys, zs = [], []
            for n in range(ORDER):
                power = wide(pw, (ct * (SEG + 1) + i + 1) * ORDER + n)
                ys.append(power * h[n])
                zs.append(power * g[n])
            while len(ys) > 1:
                ys = [a + b for a, b in zip(ys[::2], ys[1::2])]
                zs = [a + b for a, b in zip(zs[::2], zs[1::2])]
            yn[pl.ds(ct * rows + i, NSEG, stride=SEG), :] = y + ys[0]
            zn[pl.ds(ct * rows + SEG - 1 - i, NSEG, stride=SEG), :] = z + zs[0]
        cols = pl.ds(pl.multiple_of(ct * LANES, LANES), LANES)
        gain = jnp.broadcast_to(skip[:, cols], (SEG, LANES))
        for r in range(rows // SEG):
            at = (pl.ds(r * SEG, SEG), cols)
            here = pl.ds(pl.multiple_of(ct * rows + r * SEG, SEG), SEG)
            conv = yn[here, :].astype(jnp.bfloat16).astype(jnp.float32)
            adj = zn[here, :].astype(jnp.bfloat16).astype(jnp.float32)
            mixed = conv + gain * xs[here, :]
            grad = adj + gain * ps[here, :]
            op_out[at] = (q_in[at].astype(jnp.float32) * mixed).astype(jnp.bfloat16)
            gq_out[at] = (c_in[at].astype(jnp.float32) * mixed).astype(jnp.bfloat16)
            gk_out[at] = (v_in[at].astype(jnp.float32) * grad).astype(jnp.bfloat16)
            gv_out[at] = (k_in[at].astype(jnp.float32) * grad).astype(jnp.bfloat16)
        for copy in out_copies((slice(None), cols)):
            copy.start()

    half_line = OWNERS // 2

    @pl.when(early)
    def _():
        wait_bytes(column.at[pl.ds(0, half_line - 1)], recv_sems.at[3])

    @pl.when(jnp.logical_not(early))
    def _():
        wait_bytes(column, recv_sems.at[3])

    total = jnp.sum(jnp.sum(column[...], axis=0), axis=1, keepdims=True)
    factor = jnp.minimum(1.0, math.sqrt(D * ORDER) / jnp.sqrt(total + 1e-06))
    for j, (half, ct) in enumerate(pieces):
        gr_out[pl.ds(half * ROWS, ROWS), lanes(ct)] = from_owners(2, half, ct) * factor
    last = pltpu.make_async_copy(gr_out, gr_hbm, out_sems.at[4])
    last.start()
    wait_bytes(send1, send_sems.at[0])

    @pl.when(early)
    def _():
        wait_bytes(send2, send_sems.at[1])
        wait_bytes(plane.at[pl.ds(0, 2 * n_tp - 1)], send_sems.at[2])
        wait_bytes(plane.at[pl.ds(0, CTX // 2 - 1)], send_sems.at[3])

    for copy in out_copies((slice(None), slice(None))):
        copy.wait()
    last.wait()


def write(*refs):
    count = len(refs) // 2
    sems, copies = refs[-1], []
    for i in range(count):
        copies.append(pltpu.make_async_copy(refs[i], refs[count + i], sems.at[i]))
        copies[i].start()
    for copy in copies:
        copy.wait()


def shards(queries, keys_in, values_in, decay_rates, residues, skip_gain, cotangent):
    rows, chans = queries.shape
    n_tp = lax.axis_size("tp")
    cts = chans // LANES
    f32, bf16 = jnp.float32, jnp.bfloat16
    line = jax.ShapeDtypeStruct((rows, chans), bf16)
    anywhere = pl.BlockSpec(memory_space=pl.ANY)
    table = pltpu.VMEM((cts * rows, LANES), f32)
    posts = pltpu.VMEM((CTX * ROWS, LANES), f32)
    outs = pl.pallas_call(
        kernel,
        out_shape=(line, line, line, line, jax.ShapeDtypeStruct((ORDER, chans), f32)),
        in_specs=[pl.BlockSpec(memory_space=pltpu.HBM)] * 7,
        out_specs=(anywhere,) * 5,
        scratch_shapes=[
            *[pltpu.VMEM((rows, chans), bf16)] * 4,
            pltpu.VMEM((ORDER, chans), f32),
            pltpu.VMEM((ORDER, chans), f32),
            pltpu.VMEM((1, chans), f32),
            *[pltpu.VMEM((rows, chans), bf16)] * 4,
            pltpu.VMEM((ORDER, chans), f32),
            *[table] * 5,
            pltpu.VMEM((cts * (SEG + 1) * ORDER, LANES), f32),
            pltpu.VMEM((cts * (SEG + 1) * ROWS, LANES), f32),
            *[table] * 4,
            posts,
            pltpu.VMEM((CTX * PIECES * ROWS, LANES), f32),
            pltpu.VMEM((CTX * PIECES * ROWS, LANES), f32),
            posts,
            pltpu.VMEM((2 * n_tp, 1, LANES), f32),
            pltpu.VMEM((OWNERS // 2, 1, LANES), f32),
            pltpu.SemaphoreType.DMA((7,)),
            pltpu.SemaphoreType.DMA((5,)),
            pltpu.SemaphoreType.DMA((4,)),
            pltpu.SemaphoreType.DMA((4,)),
        ],
        compiler_params=pltpu.CompilerParams(collective_id=0, has_side_effects=True),
        name="modal_conv",
    )(queries, keys_in, values_in, cotangent, decay_rates.T, residues.T, skip_gain.reshape(1, chans))
    outs = pl.pallas_call(
        write,
        out_shape=tuple(jax.ShapeDtypeStruct(o.shape, o.dtype) for o in outs),
        in_specs=[anywhere] * 5,
        out_specs=(pl.BlockSpec(memory_space=pltpu.HBM),) * 5,
        scratch_shapes=[pltpu.SemaphoreType.DMA((5,))],
        name="write_out",
    )(*outs)
    return (*outs[:4], outs[4].T)


def solution(mesh):
    line, modes = P("ctx", "tp"), P("tp", None)
    in_specs = (line, line, line, modes, modes, P("tp"), line)
    out_specs = (line, line, line, line, modes)
    return jax.shard_map(shards, mesh=mesh, in_specs=in_specs, out_specs=out_specs, check_vma=False)
```

```python
import math

import jax
import jax.numpy as jnp
from jax import lax
from jax.experimental import pallas as pl
from jax.experimental.pallas import tpu as pltpu
from jax.sharding import PartitionSpec as P

D = 8192
ORDER = 16
LANES = 128
ROWS = 8
SEG = 16
NSEG = 8
CTX = 32
PLANES = 4
OWNERS = 2 * PLANES
POST = 32
MESH = pl.DeviceIdType.MESH


def kernel(
    q_hbm, k_hbm, v_hbm, c_hbm, dec_hbm, res_hbm, skip_hbm,
    op_hbm, gq_hbm, gk_hbm, gv_hbm, gr_hbm,
    q_in, k_in, v_in, c_in, dec, res, skip,
    op_out, gq_out, gk_out, gv_out, gr_out,
    xs, ps, hs, gs, far, pw, taps, yl, zl, yn, zn,
    send1, recv1, send2, recv2, rate_in, plane, column,
    in_sems, out_sems, send_sems, recv_sems,
):
    me, mt = lax.axis_index("ctx"), lax.axis_index("tp")
    n_tp = plane.shape[0] // 2
    half_ctx = CTX // 2
    upper, line = me // half_ctx, lax.rem(me, half_ctx)
    floor = line // 2

    def owner_line(up, z):
        return 2 * z + lax.rem(up + z + 1, 2)

    owner = (floor < PLANES) & (line == owner_line(upper, floor))
    there = lax.rem(mt + n_tp // 2, n_tp)
    slot = upper * PLANES + floor
    spot = upper * n_tp + mt
    rows, chans = q_in.shape
    cts = chans // LANES

    ins = [
        pltpu.make_async_copy(src, dst, in_sems.at[i])
        for i, (src, dst) in enumerate(
            zip((dec_hbm, res_hbm, skip_hbm, k_hbm, v_hbm, q_hbm, c_hbm), (dec, res, skip, k_in, v_in, q_in, c_in))
        )
    ]
    for copy in ins[3:] + ins[:3]:
        copy.start()

    barrier = pltpu.get_barrier_semaphore()

    def in_plane(off):
        other = lax.rem(spot + off, 2 * n_tp)
        up = other // n_tp
        return {"ctx": up * half_ctx + owner_line(up, floor), "tp": lax.rem(other, n_tp)}

    @pl.when(owner)
    def _():
        @pl.loop(0, CTX)
        def _(off):
            to = {"ctx": lax.rem(me + off, CTX), "tp": there}
            pl.semaphore_signal(barrier, inc=1, device_id=to, device_id_type=MESH)

        @pl.loop(1, 2 * n_tp)
        def _(off):
            pl.semaphore_signal(barrier, inc=1, device_id=in_plane(off), device_id_type=MESH)

    def lanes(ct):
        return pl.ds(ct * LANES, LANES)

    for copy in ins:
        copy.wait()

    for ct in range(cts):
        for r in range(rows // 16):
            at = (pl.ds(r * 16, 16), lanes(ct))
            to = pl.ds(ct * rows + r * 16, 16)
            kv = k_in[at].astype(jnp.float32) * v_in[at].astype(jnp.float32)
            cq = c_in[at].astype(jnp.float32) * q_in[at].astype(jnp.float32)
            xs[to, :] = kv.astype(jnp.bfloat16).astype(jnp.float32)
            ps[to, :] = cq.astype(jnp.bfloat16).astype(jnp.float32)

    pieces = [(half, ct) for half in range(2) for ct in range(cts)]
    rate = [dec[pl.ds(half * ROWS, ROWS), lanes(ct)] for half, ct in pieces]
    decay = [jnp.exp(-d) for d in rate]

    def wide(ref, row):
        return jnp.broadcast_to(ref[pl.ds(row, 1), :], (ROWS, LANES))

    zeros = [jnp.zeros((ROWS, LANES), jnp.float32) for _ in pieces]

    def scan_segment(r, state):
        fwd, inner, bwd = (list(part_) for part_ in state)
        back = NSEG - 1 - r
        for j, (half, ct) in enumerate(pieces):
            hs[pl.ds(pl.multiple_of(ct * rows + r * SEG + half * ROWS, ROWS), ROWS), :] = fwd[j]
            gs[pl.ds(pl.multiple_of(ct * rows + back * SEG + half * ROWS, ROWS), ROWS), :] = bwd[j]
        for i in range(SEG):
            for ct in range(cts):
                x = wide(xs, ct * rows + r * SEG + i)
                p = wide(ps, ct * rows + r * SEG + i)
                pb = wide(ps, ct * rows + back * SEG + (SEG - 1 - i))
                for half in range(2):
                    j = half * cts + ct
                    fwd[j] = fwd[j] * decay[j] + x
                    inner[j] = inner[j] + fwd[j] * p
                    bwd[j] = bwd[j] * decay[j] + pb
        return fwd, inner, bwd

    fwd, inner, bwd = lax.fori_loop(0, NSEG, scan_segment, (zeros, zeros, zeros))

    f32, bf16 = jnp.float32, jnp.bfloat16

    def message(first, second, sums):
        high = sums.astype(bf16)
        low = (sums - high.astype(f32)).astype(bf16)
        return jnp.concatenate([first.astype(bf16), second.astype(bf16), high, low], axis=0)

    def parts(ref, index):
        both = ref[pl.ds(index * POST, POST), :].astype(f32)
        first, second, high, low = (both[i * ROWS : (i + 1) * ROWS] for i in range(4))
        return first, second, high + low

    for j, (half, ct) in enumerate(pieces):
        send1[pl.ds((2 * ct + half) * POST, POST), :] = message(fwd[j], bwd[j], inner[j])

    def tile(index):
        return pl.ds(pl.multiple_of(index * ROWS, ROWS), ROWS)

    @pl.when(owner)
    def _():
        pl.semaphore_wait(barrier, OWNERS + 2 * n_tp - 1)

    @pl.when(jnp.logical_not(owner))
    def _():
        pl.semaphore_wait(barrier, OWNERS)

    def group(index):
        return pl.ds(pl.multiple_of(index * POST, POST), POST)

    rate_at = dec.at[
        pl.ds(pl.multiple_of(lax.rem(slot, 2) * ROWS, ROWS), ROWS),
        pl.ds(pl.multiple_of(slot // 2 * LANES, LANES), LANES),
    ]
    rate_copy = pltpu.make_async_remote_copy(
        src_ref=rate_at,
        dst_ref=rate_in,
        send_sem=send_sems.at[4],
        recv_sem=recv_sems.at[4],
        device_id={"tp": there},
        device_id_type=MESH,
    )

    @pl.when(owner)
    def _():
        rate_copy.start()

    @pl.loop(0, OWNERS)
    def _(off):
        to = lax.rem(slot + off, OWNERS)
        up, z = to // PLANES, lax.rem(to, PLANES)
        pltpu.make_async_remote_copy(
            src_ref=send1.at[group(to), :],
            dst_ref=recv1.at[group(me), :],
            send_sem=send_sems.at[0],
            recv_sem=recv_sems.at[0],
            device_id={"ctx": up * half_ctx + owner_line(up, z), "tp": there},
            device_id_type=MESH,
        ).start()

    def wait_bytes(ref, sem):
        pltpu.make_async_copy(ref, ref, sem).wait()

    unit = [jnp.sqrt(1.0 - jnp.exp(-2.0 * d)) for d in rate]
    coef = [
        res[pl.ds(half * ROWS, ROWS), lanes(ct)] * unit[j] for j, (half, ct) in enumerate(pieces)
    ]

    @pl.loop(0, SEG + 1)
    def _(i):
        lag = i.astype(jnp.float32)
        for ct in range(cts):
            total = None
            for half in range(2):
                j = half * cts + ct
                power = coef[j] * jnp.exp(-rate[j] * lag)
                pw[pl.ds(pl.multiple_of((ct * (SEG + 1) + i) * ORDER + half * ROWS, ROWS), ROWS), :] = power
                total = power if total is None else total + power
            total = jnp.sum(total, axis=0, keepdims=True)
            taps[tile(ct * (SEG + 1) + i), :] = jnp.broadcast_to(total, (ROWS, LANES))

    @pl.loop(0, NSEG)
    def _(r):
        lag = (r * SEG).astype(jnp.float32)
        for j, (half, ct) in enumerate(pieces):
            far[pl.ds(pl.multiple_of(ct * rows + r * SEG + half * ROWS, ROWS), ROWS), :] = jnp.exp(-rate[j] * lag)

    @pl.loop(0, cts)
    def _(ct):
        x = [xs[pl.ds(ct * rows + i, NSEG, stride=SEG), :] for i in range(SEG)]
        p = [ps[pl.ds(ct * rows + i, NSEG, stride=SEG), :] for i in range(SEG)]
        tap = [taps[tile(ct * (SEG + 1) + i), :] for i in range(SEG)]
        for i in range(SEG):
            y = x[i] * tap[0]
            for lag in range(1, i + 1):
                y = y + x[i - lag] * tap[lag]
            yl[tile(ct * SEG + i), :] = y
            z = p[i] * tap[0]
            for lag in range(1, SEG - i):
                z = z + p[i + lag] * tap[lag]
            zl[tile(ct * SEG + i), :] = z

    @pl.when(owner)
    def _():
        rate_copy.wait_recv()
        rates = rate_in[...]
        block = jnp.exp(-float(rows) * rates)
        step = jnp.exp(-rates)
        scale = jnp.sqrt(1.0 - jnp.exp(-2.0 * rates))
        wait_bytes(recv1, recv_sems.at[0])

        zero = jnp.zeros((ROWS, LANES), f32)
        ahead = [zero]
        cross, inside = zero, zero
        for e in range(CTX):
            start, end, own = parts(recv1, e)
            cross = cross + end * ahead[e]
            inside = inside + own
            ahead.append(ahead[e] * block + start)
        raw = scale * (inside + step * cross)

        plane[spot] = jnp.sum(raw * raw, axis=0, keepdims=True)

        @pl.loop(1, 2 * n_tp)
        def _(off):
            pltpu.make_async_remote_copy(
                src_ref=plane.at[spot],
                dst_ref=plane.at[spot],
                send_sem=send_sems.at[2],
                recv_sem=recv_sems.at[2],
                device_id=in_plane(off),
                device_id_type=MESH,
            ).start()

        carry = zero
        for e in reversed(range(CTX)):
            send2[pl.ds(e * POST, POST), :] = message(ahead[e], carry, raw)
            carry = carry * block + parts(recv1, e)[1]

        @pl.loop(0, CTX)
        def _(off):
            to = lax.rem(upper + off, 2) * half_ctx + off // 2
            pltpu.make_async_remote_copy(
                src_ref=send2.at[group(to), :],
                dst_ref=recv2.at[group(slot), :],
                send_sem=send_sems.at[1],
                recv_sem=recv_sems.at[1],
                device_id={"ctx": to, "tp": there},
                device_id_type=MESH,
            ).start()

        wait_bytes(plane.at[pl.ds(0, 2 * n_tp - 1)], recv_sems.at[2])
        column[floor] = jnp.sum(plane[...], axis=0)

        @pl.loop(1, half_ctx)
        def _(off):
            pltpu.make_async_remote_copy(
                src_ref=column.at[floor],
                dst_ref=column.at[floor],
                send_sem=send_sems.at[3],
                recv_sem=recv_sems.at[3],
                device_id={"ctx": upper * half_ctx + lax.rem(line + off, half_ctx)},
                device_id_type=MESH,
            ).start()

    wait_bytes(recv2, recv_sems.at[1])

    returned = [parts(recv2, 2 * ct + half) for half, ct in pieces]

    before = [first for first, _, _ in returned]
    after = [second for _, second, _ in returned]

    @pl.loop(0, NSEG)
    def _(r):
        for j, (half, ct) in enumerate(pieces):
            here = pl.ds(pl.multiple_of(ct * rows + r * SEG + half * ROWS, ROWS), ROWS)
            mirror = pl.ds(pl.multiple_of(ct * rows + (NSEG - 1 - r) * SEG + half * ROWS, ROWS), ROWS)
            hs[here, :] = hs[here, :] + far[here, :] * before[j]
            gs[here, :] = gs[here, :] + far[mirror, :] * after[j]

    def out_copies(at):
        return [
            pltpu.make_async_copy(src.at[at], dst.at[at], out_sems.at[i])
            for i, (src, dst) in enumerate(
                ((op_out, op_hbm), (gq_out, gq_hbm), (gk_out, gk_hbm), (gv_out, gv_hbm))
            )
        ]

    @pl.loop(0, cts)
    def _(ct):
        h = [hs[pl.ds(ct * rows + n, NSEG, stride=SEG), :] for n in range(ORDER)]
        g = [gs[pl.ds(ct * rows + n, NSEG, stride=SEG), :] for n in range(ORDER)]
        for i in range(SEG):
            y = yl[tile(ct * SEG + i), :]
            z = zl[tile(ct * SEG + SEG - 1 - i), :]
            ys, zs = [], []
            for n in range(ORDER):
                power = wide(pw, (ct * (SEG + 1) + i + 1) * ORDER + n)
                ys.append(power * h[n])
                zs.append(power * g[n])
            while len(ys) > 1:
                ys = [a + b for a, b in zip(ys[::2], ys[1::2])]
                zs = [a + b for a, b in zip(zs[::2], zs[1::2])]
            yn[pl.ds(ct * rows + i, NSEG, stride=SEG), :] = y + ys[0]
            zn[pl.ds(ct * rows + SEG - 1 - i, NSEG, stride=SEG), :] = z + zs[0]
        cols = pl.ds(pl.multiple_of(ct * LANES, LANES), LANES)
        gain = jnp.broadcast_to(skip[:, cols], (SEG, LANES))
        for r in range(rows // SEG):
            at = (pl.ds(r * SEG, SEG), cols)
            here = pl.ds(pl.multiple_of(ct * rows + r * SEG, SEG), SEG)
            conv = yn[here, :].astype(jnp.bfloat16).astype(jnp.float32)
            adj = zn[here, :].astype(jnp.bfloat16).astype(jnp.float32)
            mixed = conv + gain * xs[here, :]
            grad = adj + gain * ps[here, :]
            op_out[at] = (q_in[at].astype(jnp.float32) * mixed).astype(jnp.bfloat16)
            gq_out[at] = (c_in[at].astype(jnp.float32) * mixed).astype(jnp.bfloat16)
            gk_out[at] = (v_in[at].astype(jnp.float32) * grad).astype(jnp.bfloat16)
            gv_out[at] = (k_in[at].astype(jnp.float32) * grad).astype(jnp.bfloat16)
        for copy in out_copies((slice(None), cols)):
            copy.start()

    @pl.when(owner)
    def _():
        wait_bytes(column.at[pl.ds(0, PLANES - 1)], recv_sems.at[3])

    @pl.when(jnp.logical_not(owner))
    def _():
        wait_bytes(column, recv_sems.at[3])

    total = jnp.sum(jnp.sum(column[...], axis=0), axis=1, keepdims=True)
    factor = jnp.minimum(1.0, math.sqrt(D * ORDER) / jnp.sqrt(total + 1e-06))
    for j, (half, ct) in enumerate(pieces):
        gr_out[pl.ds(half * ROWS, ROWS), lanes(ct)] = parts(recv2, 2 * ct + half)[2] * factor
    last = pltpu.make_async_copy(gr_out, gr_hbm, out_sems.at[4])
    last.start()
    wait_bytes(send1, send_sems.at[0])

    @pl.when(owner)
    def _():
        rate_copy.wait_send()
        wait_bytes(send2, send_sems.at[1])
        wait_bytes(plane.at[pl.ds(0, 2 * n_tp - 1)], send_sems.at[2])
        wait_bytes(plane.at[pl.ds(0, CTX // 2 - 1)], send_sems.at[3])

    for copy in out_copies((slice(None), slice(None))):
        copy.wait()
    last.wait()


def write(*refs):
    count = len(refs) // 2
    sems, copies = refs[-1], []
    for i in range(count):
        copies.append(pltpu.make_async_copy(refs[i], refs[count + i], sems.at[i]))
        copies[i].start()
    for copy in copies:
        copy.wait()


def shards(queries, keys_in, values_in, decay_rates, residues, skip_gain, cotangent):
    rows, chans = queries.shape
    n_tp = lax.axis_size("tp")
    cts = chans // LANES
    f32, bf16 = jnp.float32, jnp.bfloat16
    line = pltpu.VMEM((rows, chans), bf16)
    anywhere = pl.BlockSpec(memory_space=pl.ANY)
    table = pltpu.VMEM((cts * rows, LANES), f32)
    outs = pl.pallas_call(
        kernel,
        out_shape=(line, line, line, line, pltpu.VMEM((ORDER, chans), f32)),
        in_specs=[pl.BlockSpec(memory_space=pltpu.HBM)] * 7,
        out_specs=(anywhere,) * 5,
        scratch_shapes=[
            *[pltpu.VMEM((rows, chans), bf16)] * 4,
            pltpu.VMEM((ORDER, chans), f32),
            pltpu.VMEM((ORDER, chans), f32),
            pltpu.VMEM((1, chans), f32),
            *[pltpu.VMEM((rows, chans), bf16)] * 4,
            pltpu.VMEM((ORDER, chans), f32),
            *[table] * 5,
            pltpu.VMEM((cts * (SEG + 1) * ORDER, LANES), f32),
            pltpu.VMEM((cts * (SEG + 1) * ROWS, LANES), f32),
            *[table] * 4,
            pltpu.VMEM((OWNERS * POST, LANES), bf16),
            pltpu.VMEM((CTX * POST, LANES), bf16),
            pltpu.VMEM((CTX * POST, LANES), bf16),
            pltpu.VMEM((OWNERS * POST, LANES), bf16),
            pltpu.VMEM((ROWS, LANES), f32),
            pltpu.VMEM((2 * n_tp, 1, LANES), f32),
            pltpu.VMEM((PLANES, 1, LANES), f32),
            pltpu.SemaphoreType.DMA((7,)),
            pltpu.SemaphoreType.DMA((5,)),
            pltpu.SemaphoreType.DMA((5,)),
            pltpu.SemaphoreType.DMA((5,)),
        ],
        compiler_params=pltpu.CompilerParams(collective_id=0, has_side_effects=True, vmem_limit_bytes=16 * 2**20),
        name="modal_conv",
    )(
        *[
            pltpu.with_memory_space_constraint(x, pltpu.HBM)
            for x in (queries, keys_in, values_in, cotangent, decay_rates.T, residues.T, skip_gain.reshape(1, chans))
        ]
    )
    outs = pl.pallas_call(
        write,
        out_shape=tuple(jax.ShapeDtypeStruct(o.shape, o.dtype) for o in outs),
        in_specs=[anywhere] * 5,
        out_specs=(pl.BlockSpec(memory_space=pltpu.HBM),) * 5,
        scratch_shapes=[pltpu.SemaphoreType.DMA((5,))],
        name="write_out",
        compiler_params=pltpu.CompilerParams(vmem_limit_bytes=4 * 2**20),
    )(*[pltpu.with_memory_space_constraint(x, pltpu.VMEM) for x in outs])
    return (*outs[:4], outs[4].T)


def solution(mesh):
    line, modes = P("ctx", "tp"), P("tp", None)
    in_specs = (line, line, line, modes, modes, P("tp"), line)
    out_specs = (line, line, line, line, modes)
    return jax.shard_map(shards, mesh=mesh, in_specs=in_specs, out_specs=out_specs, check_vma=False)
```

```python
import math

import jax
import jax.numpy as jnp
from jax import lax
from jax.experimental import pallas as pl
from jax.experimental.pallas import tpu as pltpu
from jax.sharding import PartitionSpec as P

D = 8192
ORDER = 16
LANES = 128
ROWS = 8
SEG = 16
NSEG = 8
CHUNKS = 4
CTX = 32
PLANES = 2
OWNERS = 2 * PLANES
POST = 3 * ORDER
BACK = 2 * ORDER
MESH = pl.DeviceIdType.MESH


def kernel(
    q_hbm, k_hbm, v_hbm, c_hbm, dec_hbm, res_hbm, skip_hbm,
    op_out, gq_out, gk_out, gv_out, gr_out,
    q_in, k_in, v_in, c_in, dec, res, skip,
    xs, ps, hs, gs, far, raf, carries, pw, taps, yl, zl, yn, zn,
    send1, recv1, send2, recv2, send3, recv3, rate_in, plane, column,
    in_sems, send_sems, recv_sems,
):
    me, mt = lax.axis_index("ctx"), lax.axis_index("tp")
    n_tp = plane.shape[0] // (2 * PLANES)
    chips = 2 * n_tp
    half_ctx = CTX // 2
    upper, line = me // half_ctx, lax.rem(me, half_ctx)
    floor = line // 2
    owner = (floor < PLANES) & (lax.rem(line, 2) == 0)
    there = lax.rem(mt + n_tp // 2, n_tp)
    slot = upper * PLANES + floor
    spot = upper * n_tp + mt
    rows, chans = q_in.shape
    cts = chans // LANES

    def fetch(src, dst, sem):
        return pltpu.make_async_copy(src, dst, sem)

    fetch(dec_hbm, dec, in_sems.at[CHUNKS]).start()
    chunk = rows // CHUNKS
    for i in range(CHUNKS):
        at = pl.ds(i * chunk, chunk)
        for src, dst in ((k_hbm, k_in), (v_hbm, v_in), (q_hbm, q_in), (c_hbm, c_in)):
            fetch(src.at[at, :], dst.at[at, :], in_sems.at[i]).start()
    fetch(res_hbm, res, in_sems.at[CHUNKS + 1]).start()
    fetch(skip_hbm, skip, in_sems.at[CHUNKS + 2]).start()

    barrier = pltpu.get_barrier_semaphore()

    ground = floor == 0

    def in_plane(index, cores, z):
        chip, core = index // cores, lax.rem(index, cores)
        return {"ctx": chip // n_tp * half_ctx + 2 * z + core, "tp": lax.rem(chip, n_tp)}

    def signal(to):
        pl.semaphore_signal(barrier, inc=1, device_id=to, device_id_type=MESH)

    @pl.when(owner)
    def _():
        @pl.loop(0, CTX)
        def _(off):
            signal({"ctx": lax.rem(me + off, CTX), "tp": there})

    is_target = ground & owner

    @pl.when(ground)
    def _():
        @pl.loop(1, chips)
        def _(off):
            signal(in_plane(lax.rem(spot + off, chips), 1, 0))

        @pl.loop(0, chips)
        def _(off):
            signal(in_plane(lax.rem(spot + off, chips), 1, 1))

        @pl.when(jnp.logical_not(owner))
        def _():
            signal(in_plane(spot, 1, 0))

    def lanes(ct):
        return pl.ds(ct * LANES, LANES)

    fetch(dec_hbm, dec, in_sems.at[CHUNKS]).wait()

    pieces = [(half, ct) for half in range(2) for ct in range(cts)]
    rate = [dec[pl.ds(half * ROWS, ROWS), lanes(ct)] for half, ct in pieces]
    decay = [jnp.exp(-d) for d in rate]

    def wide(ref, row):
        return jnp.broadcast_to(ref[pl.ds(row, 1), :], (ROWS, LANES))

    zeros = [jnp.zeros((ROWS, LANES), jnp.float32) for _ in pieces]

    block16 = [jnp.exp(-float(SEG) * d) for d in rate]

    def scan_chunk(i, state):
        fwd, inner, back, far_off = (list(part_) for part_ in state)
        fetch(k_in, k_in, in_sems.at[i]).wait()
        first = i * chunk
        for sub in range(chunk // SEG):
            for ct in range(cts):
                at = (pl.ds(pl.multiple_of(first + sub * SEG, SEG), SEG), lanes(ct))
                to = pl.ds(pl.multiple_of(ct * rows + first + sub * SEG, SEG), SEG)
                kv = k_in[at].astype(jnp.float32) * v_in[at].astype(jnp.float32)
                cq = c_in[at].astype(jnp.float32) * q_in[at].astype(jnp.float32)
                xs[to, :] = kv.astype(jnp.bfloat16).astype(jnp.float32)
                ps[to, :] = cq.astype(jnp.bfloat16).astype(jnp.float32)
        for sub in range(chunk // SEG):
            start = first + sub * SEG
            for j, (half, ct) in enumerate(pieces):
                hs[pl.ds(pl.multiple_of(ct * rows + start + half * ROWS, ROWS), ROWS), :] = fwd[j]
            own = list(zeros)
            for i2 in range(SEG):
                for ct in range(cts):
                    x = wide(xs, ct * rows + start + i2)
                    p = wide(ps, ct * rows + start + i2)
                    pb = wide(ps, ct * rows + start + (SEG - 1 - i2))
                    for half in range(2):
                        j = half * cts + ct
                        fwd[j] = fwd[j] * decay[j] + x
                        inner[j] = inner[j] + fwd[j] * p
                        own[j] = own[j] * decay[j] + pb
            for j, (half, ct) in enumerate(pieces):
                gs[pl.ds(pl.multiple_of(ct * rows + start + half * ROWS, ROWS), ROWS), :] = own[j]
                back[j] = back[j] + far_off[j] * own[j]
                far_off[j] = far_off[j] * block16[j]
        return fwd, inner, back, far_off

    ones = [jnp.ones((ROWS, LANES), jnp.float32) for _ in pieces]
    fwd, inner, bwd, _ = lax.fori_loop(0, CHUNKS, scan_chunk, (zeros, zeros, zeros, ones))

    f32, bf16 = jnp.float32, jnp.bfloat16

    for j, (half, ct) in enumerate(pieces):
        if half == 0:
            for i, states in enumerate((fwd, bwd, inner)):
                both = jnp.concatenate([states[j], states[j + cts]], axis=0)
                send1[pl.ds(ct * POST + i * ORDER, ORDER), :] = both.astype(bf16)

    def tile(index):
        return pl.ds(pl.multiple_of(index * ROWS, ROWS), ROWS)

    @pl.when(is_target)
    def _():
        pl.semaphore_wait(barrier, OWNERS + 2 * chips - 1)

    @pl.when(owner & jnp.logical_not(ground))
    def _():
        pl.semaphore_wait(barrier, OWNERS + 2 * chips)

    @pl.when(jnp.logical_not(owner))
    def _():
        pl.semaphore_wait(barrier, OWNERS)

    def group(index, size):
        return pl.ds(pl.multiple_of(index * size, size), size)

    rate_at = dec.at[:, pl.ds(pl.multiple_of(slot * LANES, LANES), LANES)]
    rate_copy = pltpu.make_async_remote_copy(
        src_ref=rate_at,
        dst_ref=rate_in,
        send_sem=send_sems.at[4],
        recv_sem=recv_sems.at[4],
        device_id={"tp": there},
        device_id_type=MESH,
    )

    @pl.when(owner)
    def _():
        rate_copy.start()

    @pl.loop(0, OWNERS)
    def _(off):
        to = lax.rem(slot + off, OWNERS)
        pltpu.make_async_remote_copy(
            src_ref=send1.at[group(to, POST), :],
            dst_ref=recv1.at[group(me, POST), :],
            send_sem=send_sems.at[0],
            recv_sem=recv_sems.at[0],
            device_id={"ctx": to // PLANES * half_ctx + 2 * lax.rem(to, PLANES), "tp": there},
            device_id_type=MESH,
        ).start()

    def wait_bytes(ref, sem):
        pltpu.make_async_copy(ref, ref, sem).wait()

    fetch(res_hbm, res, in_sems.at[CHUNKS + 1]).wait()
    fetch(skip_hbm, skip, in_sems.at[CHUNKS + 2]).wait()

    def chain_back(i, after):
        r = NSEG - 1 - i
        new = []
        for j, (half, ct) in enumerate(pieces):
            here = pl.ds(pl.multiple_of(ct * rows + r * SEG + half * ROWS, ROWS), ROWS)
            own = gs[here, :]
            gs[here, :] = after[j]
            new.append(after[j] * block16[j] + own)
        return new

    lax.fori_loop(0, NSEG, chain_back, zeros)
    unit = [jnp.sqrt(1.0 - jnp.exp(-2.0 * d)) for d in rate]
    coef = [
        res[pl.ds(half * ROWS, ROWS), lanes(ct)] * unit[j] for j, (half, ct) in enumerate(pieces)
    ]

    @pl.loop(0, SEG + 1)
    def _(i):
        lag = i.astype(jnp.float32)
        for ct in range(cts):
            total = None
            for half in range(2):
                j = half * cts + ct
                power = coef[j] * jnp.exp(-rate[j] * lag)
                pw[pl.ds(pl.multiple_of((ct * (SEG + 1) + i) * ORDER + half * ROWS, ROWS), ROWS), :] = power
                total = power if total is None else total + power
            total = jnp.sum(total, axis=0, keepdims=True)
            taps[tile(ct * (SEG + 1) + i), :] = jnp.broadcast_to(total, (ROWS, LANES))

    @pl.loop(0, NSEG)
    def _(r):
        lag = (r * SEG).astype(jnp.float32)
        for j, (half, ct) in enumerate(pieces):
            power = jnp.exp(-rate[j] * lag)
            far[pl.ds(pl.multiple_of(ct * rows + r * SEG + half * ROWS, ROWS), ROWS), :] = power
            mirror = ct * rows + (NSEG - 1 - r) * SEG + half * ROWS
            raf[pl.ds(pl.multiple_of(mirror, ROWS), ROWS), :] = power

    @pl.loop(0, cts)
    def _(ct):
        x = [xs[pl.ds(ct * rows + i, NSEG, stride=SEG), :] for i in range(SEG)]
        p = [ps[pl.ds(ct * rows + i, NSEG, stride=SEG), :] for i in range(SEG)]
        tap = [taps[tile(ct * (SEG + 1) + i), :] for i in range(SEG)]
        for i in range(SEG):
            y = x[i] * tap[0]
            for lag in range(1, i + 1):
                y = y + x[i - lag] * tap[lag]
            yl[tile(ct * SEG + i), :] = y
            z = p[i] * tap[0]
            for lag in range(1, SEG - i):
                z = z + p[i + lag] * tap[lag]
            zl[tile(ct * SEG + i), :] = z

    @pl.when(owner)
    def _():
        rate_copy.wait_recv()
        rates = rate_in[...]
        block = jnp.exp(-float(rows) * rates)
        step = jnp.exp(-rates)
        scale = jnp.sqrt(1.0 - jnp.exp(-2.0 * rates))
        wait_bytes(recv1, recv_sems.at[0])

        def came(e, i):
            return recv1[pl.ds(e * POST + i * ORDER, ORDER), :].astype(f32)

        zero = jnp.zeros((ORDER, LANES), f32)
        carry, back, cross, inside = zero, zero, zero, zero
        for e in range(CTX):
            last = CTX - 1 - e
            send2[pl.ds(e * BACK, ORDER), :] = carry.astype(bf16)
            send2[pl.ds(last * BACK + ORDER, ORDER), :] = back.astype(bf16)
            cross = cross + came(e, 1) * carry
            inside = inside + came(e, 2)
            carry = carry * block + came(e, 0)
            back = back * block + came(last, 1)
        raw = scale * (inside + step * cross)
        send3[...] = raw

        part = floor * chips + spot
        plane[part] = jnp.sum(raw * raw, axis=0, keepdims=True)

        def tell(to):
            pltpu.make_async_remote_copy(
                src_ref=plane.at[part],
                dst_ref=plane.at[part],
                send_sem=send_sems.at[2],
                recv_sem=recv_sems.at[2],
                device_id=to,
                device_id_type=MESH,
            ).start()

        @pl.loop(2, 2 * chips)
        def _(off):
            tell(in_plane(lax.rem(2 * spot + off, 2 * chips), 2, 0))

        tell(in_plane(2 * spot + 1, 2, 0))

        @pl.when(jnp.logical_not(ground))
        def _():
            tell(in_plane(2 * spot, 2, 0))

        @pl.loop(0, CTX)
        def _(off):
            to = lax.rem(upper + off, 2) * half_ctx + off // 2
            for src, dst, which in (
                (send2.at[group(to, BACK), :], recv2.at[group(slot, BACK), :], 1),
                (send3, recv3.at[group(slot, ORDER), :], 5),
            ):
                pltpu.make_async_remote_copy(
                    src_ref=src,
                    dst_ref=dst,
                    send_sem=send_sems.at[which],
                    recv_sem=recv_sems.at[which],
                    device_id={"ctx": to, "tp": there},
                    device_id_type=MESH,
                ).start()

    wait_bytes(recv2, recv_sems.at[1])

    carries[...] = recv2[...].astype(f32)

    @pl.loop(0, cts)
    def _(ct):
        def edges(near, power, n, which):
            at = pl.ds(ct * rows + n, NSEG, stride=SEG)
            return near[at, :] + power[at, :] * wide(carries, ct * BACK + which * ORDER + n)

        h = [edges(hs, far, n, 0) for n in range(ORDER)]
        g = [edges(gs, raf, n, 1) for n in range(ORDER)]
        for i in range(SEG):
            y = yl[tile(ct * SEG + i), :]
            z = zl[tile(ct * SEG + SEG - 1 - i), :]
            ys, zs = [], []
            for n in range(ORDER):
                power = wide(pw, (ct * (SEG + 1) + i + 1) * ORDER + n)
                ys.append(power * h[n])
                zs.append(power * g[n])
            while len(ys) > 1:
                ys = [a + b for a, b in zip(ys[::2], ys[1::2])]
                zs = [a + b for a, b in zip(zs[::2], zs[1::2])]
            yn[pl.ds(ct * rows + i, NSEG, stride=SEG), :] = y + ys[0]
            zn[pl.ds(ct * rows + SEG - 1 - i, NSEG, stride=SEG), :] = z + zs[0]
        cols = pl.ds(pl.multiple_of(ct * LANES, LANES), LANES)
        gain = jnp.broadcast_to(skip[:, cols], (SEG, LANES))
        for r in range(rows // SEG):
            at = (pl.ds(r * SEG, SEG), cols)
            here = pl.ds(pl.multiple_of(ct * rows + r * SEG, SEG), SEG)
            conv = yn[here, :].astype(jnp.bfloat16).astype(jnp.float32)
            adj = zn[here, :].astype(jnp.bfloat16).astype(jnp.float32)
            mixed = conv + gain * xs[here, :]
            grad = adj + gain * ps[here, :]
            op_out[at] = (q_in[at].astype(jnp.float32) * mixed).astype(jnp.bfloat16)
            gq_out[at] = (c_in[at].astype(jnp.float32) * mixed).astype(jnp.bfloat16)
            gk_out[at] = (v_in[at].astype(jnp.float32) * grad).astype(jnp.bfloat16)
            gv_out[at] = (k_in[at].astype(jnp.float32) * grad).astype(jnp.bfloat16)

    @pl.when(ground)
    def _():
        @pl.when(owner)
        def _():
            wait_bytes(plane.at[pl.ds(0, 2 * chips - 1)], recv_sems.at[2])

        @pl.when(jnp.logical_not(owner))
        def _():
            wait_bytes(plane, recv_sems.at[2])

        column[...] = jnp.sum(plane[...], axis=0)

        @pl.when(owner)
        def _():
            @pl.loop(2, half_ctx)
            def _(off):
                pltpu.make_async_remote_copy(
                    src_ref=column,
                    dst_ref=column,
                    send_sem=send_sems.at[3],
                    recv_sem=recv_sems.at[3],
                    device_id={"ctx": upper * half_ctx + off},
                    device_id_type=MESH,
                ).start()

    @pl.when(jnp.logical_not(ground))
    def _():
        wait_bytes(column, recv_sems.at[3])

    wait_bytes(recv3, recv_sems.at[5])
    total = jnp.sum(column[...], axis=1, keepdims=True)
    factor = jnp.minimum(1.0, math.sqrt(D * ORDER) / jnp.sqrt(total + 1e-06))
    for ct in range(cts):
        gr_out[:, lanes(ct)] = recv3[pl.ds(ct * ORDER, ORDER), :] * factor
    wait_bytes(send1, send_sems.at[0])

    @pl.when(owner)
    def _():
        rate_copy.wait_send()
        wait_bytes(send2, send_sems.at[1])
        wait_bytes(xs.at[pl.ds(0, CTX * ORDER), :], send_sems.at[5])

    @pl.when(is_target)
    def _():
        wait_bytes(plane.at[pl.ds(0, 2 * chips - 1)], send_sems.at[2])
        wait_bytes(plane.at[pl.ds(0, half_ctx - 2)], send_sems.at[3])

    @pl.when(owner & jnp.logical_not(ground))
    def _():
        wait_bytes(plane, send_sems.at[2])


def write(*refs):
    count = len(refs) // 2
    sems, copies = refs[-1], []
    for i in range(count):
        copies.append(pltpu.make_async_copy(refs[i], refs[count + i], sems.at[i]))
        copies[i].start()
    for copy in copies:
        copy.wait()


def shards(queries, keys_in, values_in, decay_rates, residues, skip_gain, cotangent):
    rows, chans = queries.shape
    n_tp = lax.axis_size("tp")
    cts = chans // LANES
    f32, bf16 = jnp.float32, jnp.bfloat16
    line = pltpu.VMEM((rows, chans), bf16)
    anywhere = pl.BlockSpec(memory_space=pl.ANY)
    table = pltpu.VMEM((cts * rows, LANES), f32)
    outs = pl.pallas_call(
        kernel,
        out_shape=(line, line, line, line, pltpu.VMEM((ORDER, chans), f32)),
        in_specs=[pl.BlockSpec(memory_space=pltpu.HBM)] * 7,
        out_specs=(pl.BlockSpec(memory_space=pltpu.VMEM),) * 5,
        scratch_shapes=[
            *[pltpu.VMEM((rows, chans), bf16)] * 4,
            pltpu.VMEM((ORDER, chans), f32),
            pltpu.VMEM((ORDER, chans), f32),
            pltpu.VMEM((1, chans), f32),
            *[table] * 6,
            pltpu.VMEM((OWNERS * BACK, LANES), f32),
            pltpu.VMEM((cts * (SEG + 1) * ORDER, LANES), f32),
            pltpu.VMEM((cts * (SEG + 1) * ROWS, LANES), f32),
            *[table] * 4,
            pltpu.VMEM((OWNERS * POST, LANES), bf16),
            pltpu.VMEM((CTX * POST, LANES), bf16),
            pltpu.VMEM((CTX * BACK, LANES), bf16),
            pltpu.VMEM((OWNERS * BACK, LANES), bf16),
            pltpu.VMEM((ORDER, LANES), f32),
            pltpu.VMEM((OWNERS * ORDER, LANES), f32),
            pltpu.VMEM((ORDER, LANES), f32),
            pltpu.VMEM((2 * n_tp * PLANES, 1, LANES), f32),
            pltpu.VMEM((1, LANES), f32),
            pltpu.SemaphoreType.DMA((CHUNKS + 3,)),
            pltpu.SemaphoreType.DMA((6,)),
            pltpu.SemaphoreType.DMA((6,)),
        ],
        compiler_params=pltpu.CompilerParams(collective_id=0, has_side_effects=True, vmem_limit_bytes=16 * 2**20),
        name="modal_conv",
    )(
        *[
            pltpu.with_memory_space_constraint(x, pltpu.HBM)
            for x in (queries, keys_in, values_in, cotangent, decay_rates.T, residues.T, skip_gain.reshape(1, chans))
        ]
    )
    outs = pl.pallas_call(
        write,
        out_shape=tuple(jax.ShapeDtypeStruct(o.shape, o.dtype) for o in outs),
        in_specs=[anywhere] * 5,
        out_specs=(pl.BlockSpec(memory_space=pltpu.HBM),) * 5,
        scratch_shapes=[pltpu.SemaphoreType.DMA((5,))],
        name="write_out",
        compiler_params=pltpu.CompilerParams(vmem_limit_bytes=4 * 2**20),
    )(*[pltpu.with_memory_space_constraint(x, pltpu.VMEM) for x in outs])
    return (*outs[:4], outs[4].T)


def solution(mesh):
    line, modes = P("ctx", "tp"), P("tp", None)
    in_specs = (line, line, line, modes, modes, P("tp"), line)
    out_specs = (line, line, line, line, modes)
    return jax.shard_map(shards, mesh=mesh, in_specs=in_specs, out_specs=out_specs, check_vma=False)
```

```python
import math

import jax
import jax.numpy as jnp
from jax import lax
from jax.experimental import pallas as pl
from jax.experimental.pallas import tpu as pltpu
from jax.sharding import PartitionSpec as P

D = 8192
ORDER = 16
LANES = 128
ROWS = 8
SEG = 16
NSEG = 8
CHUNKS = 4
CTX = 32
PLANES = 2
OWNERS = 2 * PLANES
POST = 3 * ORDER
BACK = 2 * ORDER
MESH = pl.DeviceIdType.MESH


def kernel(
    q_hbm, k_hbm, v_hbm, c_hbm, dec_hbm, res_hbm, skip_hbm,
    op_out, gq_out, gk_out, gv_out, gr_out,
    q_in, k_in, v_in, c_in, dec, res, skip,
    xs, ps, hs, gs, far, raf, carries, pw, taps, yl, zl, yn, zn,
    send1, recv1, send2, recv2, send3, recv3, rate_in, plane, column,
    in_sems, send_sems, recv_sems,
):
    me, mt = lax.axis_index("ctx"), lax.axis_index("tp")
    n_tp = plane.shape[0] // (2 * PLANES)
    chips = 2 * n_tp
    half_ctx = CTX // 2
    upper, line = me // half_ctx, lax.rem(me, half_ctx)
    floor = line // 2
    owner = (floor < PLANES) & (lax.rem(line, 2) == 0)
    there = lax.rem(mt + n_tp // 2, n_tp)
    slot = upper * PLANES + floor
    spot = upper * n_tp + mt
    rows, chans = q_in.shape
    cts = chans // LANES

    def fetch(src, dst, sem):
        return pltpu.make_async_copy(src, dst, sem)

    fetch(dec_hbm, dec, in_sems.at[CHUNKS]).start()
    chunk = rows // CHUNKS
    for i in range(CHUNKS):
        at = pl.ds(i * chunk, chunk)
        for src, dst in ((k_hbm, k_in), (v_hbm, v_in), (q_hbm, q_in), (c_hbm, c_in)):
            fetch(src.at[at, :], dst.at[at, :], in_sems.at[i]).start()
    fetch(res_hbm, res, in_sems.at[CHUNKS + 1]).start()
    fetch(skip_hbm, skip, in_sems.at[CHUNKS + 2]).start()

    barrier = pltpu.get_barrier_semaphore()

    ground = floor == 0

    here, over = upper * half_ctx, (1 - upper) * half_ctx

    def signal(ctx, tp):
        pl.semaphore_signal(barrier, inc=1, device_id={"ctx": ctx, "tp": tp}, device_id_type=MESH)

    @pl.when(owner)
    def _():
        @pl.loop(0, half_ctx)
        def _(off):
            signal(over + off, there)
            signal(here + off, there)

    is_target = ground & owner

    @pl.when(ground)
    def _():
        @pl.loop(1, n_tp)
        def _(off):
            tp = lax.rem(mt + off, n_tp)
            for z in range(PLANES):
                signal(over + 2 * z, tp)
                signal(here + 2 * z, tp)

        signal(over, mt)
        for z in range(1, PLANES):
            signal(over + 2 * z, mt)
            signal(here + 2 * z, mt)

        @pl.when(jnp.logical_not(owner))
        def _():
            signal(here, mt)

    def lanes(ct):
        return pl.ds(ct * LANES, LANES)

    fetch(dec_hbm, dec, in_sems.at[CHUNKS]).wait()

    pieces = [(half, ct) for half in range(2) for ct in range(cts)]
    rate = [dec[pl.ds(half * ROWS, ROWS), lanes(ct)] for half, ct in pieces]
    decay = [jnp.exp(-d) for d in rate]

    def wide(ref, row):
        return jnp.broadcast_to(ref[pl.ds(row, 1), :], (ROWS, LANES))

    zeros = [jnp.zeros((ROWS, LANES), jnp.float32) for _ in pieces]

    block16 = [jnp.exp(-float(SEG) * d) for d in rate]

    def scan_chunk(i, state):
        fwd, inner, back, far_off = (list(part_) for part_ in state)
        fetch(k_in, k_in, in_sems.at[i]).wait()
        first = i * chunk
        for sub in range(chunk // SEG):
            for ct in range(cts):
                at = (pl.ds(pl.multiple_of(first + sub * SEG, SEG), SEG), lanes(ct))
                to = pl.ds(pl.multiple_of(ct * rows + first + sub * SEG, SEG), SEG)
                kv = k_in[at].astype(jnp.float32) * v_in[at].astype(jnp.float32)
                cq = c_in[at].astype(jnp.float32) * q_in[at].astype(jnp.float32)
                xs[to, :] = kv.astype(jnp.bfloat16).astype(jnp.float32)
                ps[to, :] = cq.astype(jnp.bfloat16).astype(jnp.float32)
        for sub in range(chunk // SEG):
            start = first + sub * SEG
            for j, (half, ct) in enumerate(pieces):
                hs[pl.ds(pl.multiple_of(ct * rows + start + half * ROWS, ROWS), ROWS), :] = fwd[j]
            own = list(zeros)
            for i2 in range(SEG):
                for ct in range(cts):
                    x = wide(xs, ct * rows + start + i2)
                    p = wide(ps, ct * rows + start + i2)
                    pb = wide(ps, ct * rows + start + (SEG - 1 - i2))
                    for half in range(2):
                        j = half * cts + ct
                        fwd[j] = fwd[j] * decay[j] + x
                        inner[j] = inner[j] + fwd[j] * p
                        own[j] = own[j] * decay[j] + pb
            for j, (half, ct) in enumerate(pieces):
                gs[pl.ds(pl.multiple_of(ct * rows + start + half * ROWS, ROWS), ROWS), :] = own[j]
                back[j] = back[j] + far_off[j] * own[j]
                far_off[j] = far_off[j] * block16[j]
        return fwd, inner, back, far_off

    ones = [jnp.ones((ROWS, LANES), jnp.float32) for _ in pieces]
    fwd, inner, bwd, _ = lax.fori_loop(0, CHUNKS, scan_chunk, (zeros, zeros, zeros, ones))

    f32, bf16 = jnp.float32, jnp.bfloat16

    for j, (half, ct) in enumerate(pieces):
        if half == 0:
            for i, states in enumerate((fwd, bwd, inner)):
                both = jnp.concatenate([states[j], states[j + cts]], axis=0)
                send1[pl.ds(ct * POST + i * ORDER, ORDER), :] = both.astype(bf16)

    def tile(index):
        return pl.ds(pl.multiple_of(index * ROWS, ROWS), ROWS)

    @pl.when(is_target)
    def _():
        pl.semaphore_wait(barrier, OWNERS + 2 * chips - 1)

    @pl.when(owner & jnp.logical_not(ground))
    def _():
        pl.semaphore_wait(barrier, OWNERS + 2 * chips)

    @pl.when(jnp.logical_not(owner))
    def _():
        pl.semaphore_wait(barrier, OWNERS)

    def group(index, size):
        return pl.ds(pl.multiple_of(index * size, size), size)

    rate_at = dec.at[:, pl.ds(pl.multiple_of(slot * LANES, LANES), LANES)]
    rate_copy = pltpu.make_async_remote_copy(
        src_ref=rate_at,
        dst_ref=rate_in,
        send_sem=send_sems.at[4],
        recv_sem=recv_sems.at[4],
        device_id={"tp": there},
        device_id_type=MESH,
    )

    @pl.when(owner)
    def _():
        rate_copy.start()

    for half_at in (over, here):
        for z in reversed(range(PLANES)):
            to = half_at // half_ctx * PLANES + z
            pltpu.make_async_remote_copy(
                src_ref=send1.at[group(to, POST), :],
                dst_ref=recv1.at[group(me, POST), :],
                send_sem=send_sems.at[0],
                recv_sem=recv_sems.at[0],
                device_id={"ctx": half_at + 2 * z, "tp": there},
                device_id_type=MESH,
            ).start()

    def wait_bytes(ref, sem):
        pltpu.make_async_copy(ref, ref, sem).wait()

    fetch(res_hbm, res, in_sems.at[CHUNKS + 1]).wait()
    fetch(skip_hbm, skip, in_sems.at[CHUNKS + 2]).wait()

    def chain_back(i, after):
        r = NSEG - 1 - i
        new = []
        for j, (half, ct) in enumerate(pieces):
            here = pl.ds(pl.multiple_of(ct * rows + r * SEG + half * ROWS, ROWS), ROWS)
            own = gs[here, :]
            gs[here, :] = after[j]
            new.append(after[j] * block16[j] + own)
        return new

    lax.fori_loop(0, NSEG, chain_back, zeros)
    unit = [jnp.sqrt(1.0 - jnp.exp(-2.0 * d)) for d in rate]
    coef = [
        res[pl.ds(half * ROWS, ROWS), lanes(ct)] * unit[j] for j, (half, ct) in enumerate(pieces)
    ]

    @pl.loop(0, SEG + 1)
    def _(i):
        lag = i.astype(jnp.float32)
        for ct in range(cts):
            total = None
            for half in range(2):
                j = half * cts + ct
                power = coef[j] * jnp.exp(-rate[j] * lag)
                pw[pl.ds(pl.multiple_of((ct * (SEG + 1) + i) * ORDER + half * ROWS, ROWS), ROWS), :] = power
                total = power if total is None else total + power
            total = jnp.sum(total, axis=0, keepdims=True)
            taps[tile(ct * (SEG + 1) + i), :] = jnp.broadcast_to(total, (ROWS, LANES))

    @pl.loop(0, NSEG)
    def _(r):
        lag = (r * SEG).astype(jnp.float32)
        for j, (half, ct) in enumerate(pieces):
            power = jnp.exp(-rate[j] * lag)
            far[pl.ds(pl.multiple_of(ct * rows + r * SEG + half * ROWS, ROWS), ROWS), :] = power
            mirror = ct * rows + (NSEG - 1 - r) * SEG + half * ROWS
            raf[pl.ds(pl.multiple_of(mirror, ROWS), ROWS), :] = power

    @pl.loop(0, cts)
    def _(ct):
        x = [xs[pl.ds(ct * rows + i, NSEG, stride=SEG), :] for i in range(SEG)]
        p = [ps[pl.ds(ct * rows + i, NSEG, stride=SEG), :] for i in range(SEG)]
        tap = [taps[tile(ct * (SEG + 1) + i), :] for i in range(SEG)]
        for i in range(SEG):
            y = x[i] * tap[0]
            for lag in range(1, i + 1):
                y = y + x[i - lag] * tap[lag]
            yl[tile(ct * SEG + i), :] = y
            z = p[i] * tap[0]
            for lag in range(1, SEG - i):
                z = z + p[i + lag] * tap[lag]
            zl[tile(ct * SEG + i), :] = z

    @pl.when(owner)
    def _():
        rate_copy.wait_recv()
        rates = rate_in[...]
        block = jnp.exp(-float(rows) * rates)
        step = jnp.exp(-rates)
        scale = jnp.sqrt(1.0 - jnp.exp(-2.0 * rates))
        wait_bytes(recv1, recv_sems.at[0])

        def came(e, i):
            return recv1[pl.ds(e * POST + i * ORDER, ORDER), :].astype(f32)

        zero = jnp.zeros((ORDER, LANES), f32)
        carry, back, cross, inside = zero, zero, zero, zero
        for e in range(CTX):
            last = CTX - 1 - e
            send2[pl.ds(e * BACK, ORDER), :] = carry.astype(bf16)
            send2[pl.ds(last * BACK + ORDER, ORDER), :] = back.astype(bf16)
            cross = cross + came(e, 1) * carry
            inside = inside + came(e, 2)
            carry = carry * block + came(e, 0)
            back = back * block + came(last, 1)
        raw = scale * (inside + step * cross)
        send3[...] = raw

        part = floor * chips + spot
        plane[part] = jnp.sum(raw * raw, axis=0, keepdims=True)

        def tell(ctx, tp):
            pltpu.make_async_remote_copy(
                src_ref=plane.at[part],
                dst_ref=plane.at[part],
                send_sem=send_sems.at[2],
                recv_sem=recv_sems.at[2],
                device_id={"ctx": ctx, "tp": tp},
                device_id_type=MESH,
            ).start()

        @pl.loop(1, n_tp)
        def _(off):
            tp = lax.rem(mt + off, n_tp)
            for half_at in (over, here):
                for core in range(2):
                    tell(half_at + core, tp)

        tell(over, mt)
        tell(over + 1, mt)
        tell(here + 1, mt)

        @pl.when(jnp.logical_not(ground))
        def _():
            tell(here, mt)

        @pl.loop(0, half_ctx)
        def _(off):
            for half_at in (over, here):
                to = half_at + off
                for src, dst, which in (
                    (send2.at[group(to, BACK), :], recv2.at[group(slot, BACK), :], 1),
                    (send3, recv3.at[group(slot, ORDER), :], 5),
                ):
                    pltpu.make_async_remote_copy(
                        src_ref=src,
                        dst_ref=dst,
                        send_sem=send_sems.at[which],
                        recv_sem=recv_sems.at[which],
                        device_id={"ctx": to, "tp": there},
                        device_id_type=MESH,
                    ).start()

    wait_bytes(recv2, recv_sems.at[1])

    carries[...] = recv2[...].astype(f32)

    @pl.loop(0, cts)
    def _(ct):
        def edges(near, power, n, which):
            at = pl.ds(ct * rows + n, NSEG, stride=SEG)
            return near[at, :] + power[at, :] * wide(carries, ct * BACK + which * ORDER + n)

        h = [edges(hs, far, n, 0) for n in range(ORDER)]
        g = [edges(gs, raf, n, 1) for n in range(ORDER)]
        for i in range(SEG):
            y = yl[tile(ct * SEG + i), :]
            z = zl[tile(ct * SEG + SEG - 1 - i), :]
            ys, zs = [], []
            for n in range(ORDER):
                power = wide(pw, (ct * (SEG + 1) + i + 1) * ORDER + n)
                ys.append(power * h[n])
                zs.append(power * g[n])
            while len(ys) > 1:
                ys = [a + b for a, b in zip(ys[::2], ys[1::2])]
                zs = [a + b for a, b in zip(zs[::2], zs[1::2])]
            yn[pl.ds(ct * rows + i, NSEG, stride=SEG), :] = y + ys[0]
            zn[pl.ds(ct * rows + SEG - 1 - i, NSEG, stride=SEG), :] = z + zs[0]
        cols = pl.ds(pl.multiple_of(ct * LANES, LANES), LANES)
        gain = jnp.broadcast_to(skip[:, cols], (SEG, LANES))
        for r in range(rows // SEG):
            at = (pl.ds(r * SEG, SEG), cols)
            here = pl.ds(pl.multiple_of(ct * rows + r * SEG, SEG), SEG)
            conv = yn[here, :].astype(jnp.bfloat16).astype(jnp.float32)
            adj = zn[here, :].astype(jnp.bfloat16).astype(jnp.float32)
            mixed = conv + gain * xs[here, :]
            grad = adj + gain * ps[here, :]
            op_out[at] = (q_in[at].astype(jnp.float32) * mixed).astype(jnp.bfloat16)
            gq_out[at] = (c_in[at].astype(jnp.float32) * mixed).astype(jnp.bfloat16)
            gk_out[at] = (v_in[at].astype(jnp.float32) * grad).astype(jnp.bfloat16)
            gv_out[at] = (k_in[at].astype(jnp.float32) * grad).astype(jnp.bfloat16)

    @pl.when(ground)
    def _():
        @pl.when(owner)
        def _():
            wait_bytes(plane.at[pl.ds(0, 2 * chips - 1)], recv_sems.at[2])

        @pl.when(jnp.logical_not(owner))
        def _():
            wait_bytes(plane, recv_sems.at[2])

        column[...] = jnp.sum(plane[...], axis=0)

        @pl.when(owner)
        def _():
            @pl.loop(2, half_ctx)
            def _(off):
                pltpu.make_async_remote_copy(
                    src_ref=column,
                    dst_ref=column,
                    send_sem=send_sems.at[3],
                    recv_sem=recv_sems.at[3],
                    device_id={"ctx": here + off},
                    device_id_type=MESH,
                ).start()

    @pl.when(jnp.logical_not(ground))
    def _():
        wait_bytes(column, recv_sems.at[3])

    wait_bytes(recv3, recv_sems.at[5])
    total = jnp.sum(column[...], axis=1, keepdims=True)
    factor = jnp.minimum(1.0, math.sqrt(D * ORDER) / jnp.sqrt(total + 1e-06))
    for ct in range(cts):
        gr_out[:, lanes(ct)] = recv3[pl.ds(ct * ORDER, ORDER), :] * factor
    wait_bytes(send1, send_sems.at[0])

    @pl.when(owner)
    def _():
        rate_copy.wait_send()
        wait_bytes(send2, send_sems.at[1])
        wait_bytes(xs.at[pl.ds(0, CTX * ORDER), :], send_sems.at[5])

    @pl.when(is_target)
    def _():
        wait_bytes(plane.at[pl.ds(0, 2 * chips - 1)], send_sems.at[2])
        wait_bytes(plane.at[pl.ds(0, half_ctx - 2)], send_sems.at[3])

    @pl.when(owner & jnp.logical_not(ground))
    def _():
        wait_bytes(plane, send_sems.at[2])


def write(*refs):
    count = len(refs) // 2
    sems, copies = refs[-1], []
    for i in range(count):
        copies.append(pltpu.make_async_copy(refs[i], refs[count + i], sems.at[i]))
        copies[i].start()
    for copy in copies:
        copy.wait()


def shards(queries, keys_in, values_in, decay_rates, residues, skip_gain, cotangent):
    rows, chans = queries.shape
    n_tp = lax.axis_size("tp")
    cts = chans // LANES
    f32, bf16 = jnp.float32, jnp.bfloat16
    line = pltpu.VMEM((rows, chans), bf16)
    anywhere = pl.BlockSpec(memory_space=pl.ANY)
    table = pltpu.VMEM((cts * rows, LANES), f32)
    outs = pl.pallas_call(
        kernel,
        out_shape=(line, line, line, line, pltpu.VMEM((ORDER, chans), f32)),
        in_specs=[pl.BlockSpec(memory_space=pltpu.HBM)] * 7,
        out_specs=(pl.BlockSpec(memory_space=pltpu.VMEM),) * 5,
        scratch_shapes=[
            *[pltpu.VMEM((rows, chans), bf16)] * 4,
            pltpu.VMEM((ORDER, chans), f32),
            pltpu.VMEM((ORDER, chans), f32),
            pltpu.VMEM((1, chans), f32),
            *[table] * 6,
            pltpu.VMEM((OWNERS * BACK, LANES), f32),
            pltpu.VMEM((cts * (SEG + 1) * ORDER, LANES), f32),
            pltpu.VMEM((cts * (SEG + 1) * ROWS, LANES), f32),
            *[table] * 4,
            pltpu.VMEM((OWNERS * POST, LANES), bf16),
            pltpu.VMEM((CTX * POST, LANES), bf16),
            pltpu.VMEM((CTX * BACK, LANES), bf16),
            pltpu.VMEM((OWNERS * BACK, LANES), bf16),
            pltpu.VMEM((ORDER, LANES), f32),
            pltpu.VMEM((OWNERS * ORDER, LANES), f32),
            pltpu.VMEM((ORDER, LANES), f32),
            pltpu.VMEM((2 * n_tp * PLANES, 1, LANES), f32),
            pltpu.VMEM((1, LANES), f32),
            pltpu.SemaphoreType.DMA((CHUNKS + 3,)),
            pltpu.SemaphoreType.DMA((6,)),
            pltpu.SemaphoreType.DMA((6,)),
        ],
        compiler_params=pltpu.CompilerParams(collective_id=0, has_side_effects=True, vmem_limit_bytes=16 * 2**20),
        name="modal_conv",
    )(
        *[
            pltpu.with_memory_space_constraint(x, pltpu.HBM)
            for x in (queries, keys_in, values_in, cotangent, decay_rates.T, residues.T, skip_gain.reshape(1, chans))
        ]
    )
    outs = pl.pallas_call(
        write,
        out_shape=tuple(jax.ShapeDtypeStruct(o.shape, o.dtype) for o in outs),
        in_specs=[anywhere] * 5,
        out_specs=(pl.BlockSpec(memory_space=pltpu.HBM),) * 5,
        scratch_shapes=[pltpu.SemaphoreType.DMA((5,))],
        name="write_out",
        compiler_params=pltpu.CompilerParams(vmem_limit_bytes=4 * 2**20),
    )(*[pltpu.with_memory_space_constraint(x, pltpu.VMEM) for x in outs])
    return (*outs[:4], outs[4].T)


def solution(mesh):
    line, modes = P("ctx", "tp"), P("tp", None)
    in_specs = (line, line, line, modes, modes, P("tp"), line)
    out_specs = (line, line, line, line, modes)
    return jax.shard_map(shards, mesh=mesh, in_specs=in_specs, out_specs=out_specs, check_vma=False)
```

```python
import math

import jax
import jax.numpy as jnp
from jax import lax
from jax.experimental import pallas as pl
from jax.experimental.pallas import tpu as pltpu
from jax.sharding import PartitionSpec as P

D = 8192
ORDER = 16
LANES = 128
ROWS = 8
SEG = 16
NSEG = 8
CHUNKS = 4
CTX = 32
PLANES = 2
OWNERS = 2 * PLANES
POST = 3 * ORDER
BACK = 2 * ORDER
MESH = pl.DeviceIdType.MESH


def kernel(
    q_hbm, k_hbm, v_hbm, c_hbm, dec_hbm, res_hbm, skip_hbm,
    op_out, gq_out, gk_out, gv_out, gr_out,
    q_in, k_in, v_in, c_in, dec, res, skip,
    xs, ps, hs, gs, far, raf, carries, pw, taps, yl, zl, yn, zn,
    send1, recv1, send2, recv2, send3, recv3, rate_in, plane, column,
    in_sems, send_sems, recv_sems,
):
    me, mt = lax.axis_index("ctx"), lax.axis_index("tp")
    n_tp = plane.shape[0] // (2 * PLANES)
    chips = 2 * n_tp
    half_ctx = CTX // 2
    upper, line = me // half_ctx, lax.rem(me, half_ctx)
    floor = line // 2
    owner = (floor < PLANES) & (lax.rem(line, 2) == 0)
    there = lax.rem(mt + n_tp // 2, n_tp)
    slot = upper * PLANES + floor
    rows, chans = q_in.shape
    cts = chans // LANES

    def fetch(src, dst, sem):
        return pltpu.make_async_copy(src, dst, sem)

    fetch(dec_hbm, dec, in_sems.at[CHUNKS]).start()
    chunk = rows // CHUNKS
    for i in range(CHUNKS):
        at = pl.ds(i * chunk, chunk)
        for src, dst in ((k_hbm, k_in), (v_hbm, v_in), (q_hbm, q_in), (c_hbm, c_in)):
            fetch(src.at[at, :], dst.at[at, :], in_sems.at[i]).start()
    fetch(res_hbm, res, in_sems.at[CHUNKS + 1]).start()
    fetch(skip_hbm, skip, in_sems.at[CHUNKS + 2]).start()

    barrier = pltpu.get_barrier_semaphore()

    head = line == 1

    here, over = upper * half_ctx, (1 - upper) * half_ctx

    def signal(ctx, tp):
        pl.semaphore_signal(barrier, inc=1, device_id={"ctx": ctx, "tp": tp}, device_id_type=MESH)

    @pl.when(owner)
    def _():
        @pl.loop(0, half_ctx)
        def _(off):
            signal(over + off, there)
            signal(here + off, there)

    @pl.when(head)
    def _():
        @pl.loop(0, n_tp)
        def _(off):
            tp = lax.rem(mt + off, n_tp)
            for z in range(PLANES):
                signal(over + 2 * z, tp)
                signal(here + 2 * z, tp)

    def lanes(ct):
        return pl.ds(ct * LANES, LANES)

    fetch(dec_hbm, dec, in_sems.at[CHUNKS]).wait()

    pieces = [(half, ct) for half in range(2) for ct in range(cts)]
    rate = [dec[pl.ds(half * ROWS, ROWS), lanes(ct)] for half, ct in pieces]
    decay = [jnp.exp(-d) for d in rate]

    def wide(ref, row):
        return jnp.broadcast_to(ref[pl.ds(row, 1), :], (ROWS, LANES))

    zeros = [jnp.zeros((ROWS, LANES), jnp.float32) for _ in pieces]

    block16 = [jnp.exp(-float(SEG) * d) for d in rate]

    def scan_chunk(i, state):
        fwd, inner, back, far_off = (list(part_) for part_ in state)
        fetch(k_in, k_in, in_sems.at[i]).wait()
        first = i * chunk
        for sub in range(chunk // SEG):
            for ct in range(cts):
                at = (pl.ds(pl.multiple_of(first + sub * SEG, SEG), SEG), lanes(ct))
                to = pl.ds(pl.multiple_of(ct * rows + first + sub * SEG, SEG), SEG)
                kv = k_in[at].astype(jnp.float32) * v_in[at].astype(jnp.float32)
                cq = c_in[at].astype(jnp.float32) * q_in[at].astype(jnp.float32)
                xs[to, :] = kv.astype(jnp.bfloat16).astype(jnp.float32)
                ps[to, :] = cq.astype(jnp.bfloat16).astype(jnp.float32)
        for sub in range(chunk // SEG):
            start = first + sub * SEG
            for j, (half, ct) in enumerate(pieces):
                hs[pl.ds(pl.multiple_of(ct * rows + start + half * ROWS, ROWS), ROWS), :] = fwd[j]
            own = list(zeros)
            for i2 in range(SEG):
                for ct in range(cts):
                    x = wide(xs, ct * rows + start + i2)
                    p = wide(ps, ct * rows + start + i2)
                    pb = wide(ps, ct * rows + start + (SEG - 1 - i2))
                    for half in range(2):
                        j = half * cts + ct
                        fwd[j] = fwd[j] * decay[j] + x
                        inner[j] = inner[j] + fwd[j] * p
                        own[j] = own[j] * decay[j] + pb
            for j, (half, ct) in enumerate(pieces):
                gs[pl.ds(pl.multiple_of(ct * rows + start + half * ROWS, ROWS), ROWS), :] = own[j]
                back[j] = back[j] + far_off[j] * own[j]
                far_off[j] = far_off[j] * block16[j]
        return fwd, inner, back, far_off

    ones = [jnp.ones((ROWS, LANES), jnp.float32) for _ in pieces]
    fwd, inner, bwd, _ = lax.fori_loop(0, CHUNKS, scan_chunk, (zeros, zeros, zeros, ones))

    f32, bf16 = jnp.float32, jnp.bfloat16

    for j, (half, ct) in enumerate(pieces):
        if half == 0:
            for i, states in enumerate((fwd, bwd, inner)):
                both = jnp.concatenate([states[j], states[j + cts]], axis=0)
                send1[pl.ds(ct * POST + i * ORDER, ORDER), :] = both.astype(bf16)

    def tile(index):
        return pl.ds(pl.multiple_of(index * ROWS, ROWS), ROWS)

    @pl.when(owner)
    def _():
        pl.semaphore_wait(barrier, OWNERS + chips)

    @pl.when(jnp.logical_not(owner))
    def _():
        pl.semaphore_wait(barrier, OWNERS)

    def group(index, size):
        return pl.ds(pl.multiple_of(index * size, size), size)

    rate_at = dec.at[:, pl.ds(pl.multiple_of(slot * LANES, LANES), LANES)]
    rate_copy = pltpu.make_async_remote_copy(
        src_ref=rate_at,
        dst_ref=rate_in,
        send_sem=send_sems.at[4],
        recv_sem=recv_sems.at[4],
        device_id={"tp": there},
        device_id_type=MESH,
    )

    @pl.when(owner)
    def _():
        rate_copy.start()

    for half_at in (over, here):
        for z in reversed(range(PLANES)):
            to = half_at // half_ctx * PLANES + z
            pltpu.make_async_remote_copy(
                src_ref=send1.at[group(to, POST), :],
                dst_ref=recv1.at[group(me, POST), :],
                send_sem=send_sems.at[0],
                recv_sem=recv_sems.at[0],
                device_id={"ctx": half_at + 2 * z, "tp": there},
                device_id_type=MESH,
            ).start()

    def wait_bytes(ref, sem):
        pltpu.make_async_copy(ref, ref, sem).wait()

    fetch(res_hbm, res, in_sems.at[CHUNKS + 1]).wait()
    fetch(skip_hbm, skip, in_sems.at[CHUNKS + 2]).wait()

    def chain_back(i, after):
        r = NSEG - 1 - i
        new = []
        for j, (half, ct) in enumerate(pieces):
            here = pl.ds(pl.multiple_of(ct * rows + r * SEG + half * ROWS, ROWS), ROWS)
            own = gs[here, :]
            gs[here, :] = after[j]
            new.append(after[j] * block16[j] + own)
        return new

    lax.fori_loop(0, NSEG, chain_back, zeros)
    unit = [jnp.sqrt(1.0 - jnp.exp(-2.0 * d)) for d in rate]
    coef = [
        res[pl.ds(half * ROWS, ROWS), lanes(ct)] * unit[j] for j, (half, ct) in enumerate(pieces)
    ]

    @pl.loop(0, SEG + 1)
    def _(i):
        lag = i.astype(jnp.float32)
        for ct in range(cts):
            total = None
            for half in range(2):
                j = half * cts + ct
                power = coef[j] * jnp.exp(-rate[j] * lag)
                pw[pl.ds(pl.multiple_of((ct * (SEG + 1) + i) * ORDER + half * ROWS, ROWS), ROWS), :] = power
                total = power if total is None else total + power
            total = jnp.sum(total, axis=0, keepdims=True)
            taps[tile(ct * (SEG + 1) + i), :] = jnp.broadcast_to(total, (ROWS, LANES))

    @pl.loop(0, NSEG)
    def _(r):
        lag = (r * SEG).astype(jnp.float32)
        for j, (half, ct) in enumerate(pieces):
            power = jnp.exp(-rate[j] * lag)
            far[pl.ds(pl.multiple_of(ct * rows + r * SEG + half * ROWS, ROWS), ROWS), :] = power
            mirror = ct * rows + (NSEG - 1 - r) * SEG + half * ROWS
            raf[pl.ds(pl.multiple_of(mirror, ROWS), ROWS), :] = power

    @pl.loop(0, cts)
    def _(ct):
        x = [xs[pl.ds(ct * rows + i, NSEG, stride=SEG), :] for i in range(SEG)]
        p = [ps[pl.ds(ct * rows + i, NSEG, stride=SEG), :] for i in range(SEG)]
        tap = [taps[tile(ct * (SEG + 1) + i), :] for i in range(SEG)]
        for i in range(SEG):
            y = x[i] * tap[0]
            for lag in range(1, i + 1):
                y = y + x[i - lag] * tap[lag]
            yl[tile(ct * SEG + i), :] = y
            z = p[i] * tap[0]
            for lag in range(1, SEG - i):
                z = z + p[i + lag] * tap[lag]
            zl[tile(ct * SEG + i), :] = z

    @pl.when(owner)
    def _():
        rate_copy.wait_recv()
        rates = rate_in[...]
        block = jnp.exp(-float(rows) * rates)
        step = jnp.exp(-rates)
        scale = jnp.sqrt(1.0 - jnp.exp(-2.0 * rates))
        wait_bytes(recv1, recv_sems.at[0])

        def came(e, i):
            return recv1[pl.ds(e * POST + i * ORDER, ORDER), :].astype(f32)

        zero = jnp.zeros((ORDER, LANES), f32)
        carry, cross, inside = zero, zero, zero
        for e in range(CTX):
            send2[pl.ds(e * BACK, ORDER), :] = carry.astype(bf16)
            cross = cross + came(e, 1) * carry
            inside = inside + came(e, 2)
            carry = carry * block + came(e, 0)
        raw = scale * (inside + step * cross)
        send3[...] = raw

        part = (upper * PLANES + floor) * n_tp + mt
        plane[part] = jnp.sum(raw * raw, axis=0, keepdims=True)

        def tell(ctx, tp):
            pltpu.make_async_remote_copy(
                src_ref=plane.at[part],
                dst_ref=plane.at[part],
                send_sem=send_sems.at[2],
                recv_sem=recv_sems.at[2],
                device_id={"ctx": ctx, "tp": tp},
                device_id_type=MESH,
            ).start()

        for half_at in (0, half_ctx):

            @pl.loop(0, n_tp)
            def _(tp):
                tell(half_at + 1, tp)

        carry = zero
        for e in reversed(range(CTX)):
            send2[pl.ds(e * BACK + ORDER, ORDER), :] = carry.astype(bf16)
            carry = carry * block + came(e, 1)

        @pl.loop(0, half_ctx)
        def _(off):
            for half_at in (over, here):
                to = half_at + off
                for src, dst, which in (
                    (send2.at[group(to, BACK), :], recv2.at[group(slot, BACK), :], 1),
                    (send3, recv3.at[group(slot, ORDER), :], 5),
                ):
                    pltpu.make_async_remote_copy(
                        src_ref=src,
                        dst_ref=dst,
                        send_sem=send_sems.at[which],
                        recv_sem=recv_sems.at[which],
                        device_id={"ctx": to, "tp": there},
                        device_id_type=MESH,
                    ).start()

    wait_bytes(recv2, recv_sems.at[1])

    carries[...] = recv2[...].astype(f32)

    @pl.loop(0, cts)
    def _(ct):
        def edges(near, power, n, which):
            at = pl.ds(ct * rows + n, NSEG, stride=SEG)
            return near[at, :] + power[at, :] * wide(carries, ct * BACK + which * ORDER + n)

        h = [edges(hs, far, n, 0) for n in range(ORDER)]
        g = [edges(gs, raf, n, 1) for n in range(ORDER)]
        for i in range(SEG):
            y = yl[tile(ct * SEG + i), :]
            z = zl[tile(ct * SEG + SEG - 1 - i), :]
            ys, zs = [], []
            for n in range(ORDER):
                power = wide(pw, (ct * (SEG + 1) + i + 1) * ORDER + n)
                ys.append(power * h[n])
                zs.append(power * g[n])
            while len(ys) > 1:
                ys = [a + b for a, b in zip(ys[::2], ys[1::2])]
                zs = [a + b for a, b in zip(zs[::2], zs[1::2])]
            yn[pl.ds(ct * rows + i, NSEG, stride=SEG), :] = y + ys[0]
            zn[pl.ds(ct * rows + SEG - 1 - i, NSEG, stride=SEG), :] = z + zs[0]
        cols = pl.ds(pl.multiple_of(ct * LANES, LANES), LANES)
        gain = jnp.broadcast_to(skip[:, cols], (SEG, LANES))
        for r in range(rows // SEG):
            at = (pl.ds(r * SEG, SEG), cols)
            here = pl.ds(pl.multiple_of(ct * rows + r * SEG, SEG), SEG)
            conv = yn[here, :].astype(jnp.bfloat16).astype(jnp.float32)
            adj = zn[here, :].astype(jnp.bfloat16).astype(jnp.float32)
            mixed = conv + gain * xs[here, :]
            grad = adj + gain * ps[here, :]
            op_out[at] = (q_in[at].astype(jnp.float32) * mixed).astype(jnp.bfloat16)
            gq_out[at] = (c_in[at].astype(jnp.float32) * mixed).astype(jnp.bfloat16)
            gk_out[at] = (v_in[at].astype(jnp.float32) * grad).astype(jnp.bfloat16)
            gv_out[at] = (k_in[at].astype(jnp.float32) * grad).astype(jnp.bfloat16)

    @pl.when(head)
    def _():
        wait_bytes(plane, recv_sems.at[2])
        sums = [plane[i] for i in range(n_tp * 2 * PLANES)]
        while len(sums) > 1:
            sums = [a + b for a, b in zip(sums[::2], sums[1::2])]
        column[...] = sums[0]

        def hand(to):
            pltpu.make_async_remote_copy(
                src_ref=column,
                dst_ref=column,
                send_sem=send_sems.at[3],
                recv_sem=recv_sems.at[3],
                device_id={"ctx": to},
                device_id_type=MESH,
            ).start()

        @pl.loop(2, half_ctx)
        def _(off):
            hand(here + off)

        hand(here)

    @pl.when(jnp.logical_not(head))
    def _():
        wait_bytes(column, recv_sems.at[3])

    wait_bytes(recv3, recv_sems.at[5])
    total = jnp.sum(column[...], axis=1, keepdims=True)
    factor = jnp.minimum(1.0, math.sqrt(D * ORDER) / jnp.sqrt(total + 1e-06))
    for ct in range(cts):
        gr_out[:, lanes(ct)] = recv3[pl.ds(ct * ORDER, ORDER), :] * factor
    wait_bytes(send1, send_sems.at[0])

    @pl.when(owner)
    def _():
        rate_copy.wait_send()
        wait_bytes(send2, send_sems.at[1])
        wait_bytes(xs.at[pl.ds(0, CTX * ORDER), :], send_sems.at[5])
        wait_bytes(plane.at[pl.ds(0, chips)], send_sems.at[2])

    @pl.when(head)
    def _():
        wait_bytes(plane.at[pl.ds(0, half_ctx - 1)], send_sems.at[3])


def write(*refs):
    count = len(refs) // 2
    sems, copies = refs[-1], []
    for i in range(count):
        copies.append(pltpu.make_async_copy(refs[i], refs[count + i], sems.at[i]))
        copies[i].start()
    for copy in copies:
        copy.wait()


def shards(queries, keys_in, values_in, decay_rates, residues, skip_gain, cotangent):
    rows, chans = queries.shape
    n_tp = lax.axis_size("tp")
    cts = chans // LANES
    f32, bf16 = jnp.float32, jnp.bfloat16
    line = pltpu.VMEM((rows, chans), bf16)
    anywhere = pl.BlockSpec(memory_space=pl.ANY)
    table = pltpu.VMEM((cts * rows, LANES), f32)
    outs = pl.pallas_call(
        kernel,
        out_shape=(line, line, line, line, pltpu.VMEM((ORDER, chans), f32)),
        in_specs=[pl.BlockSpec(memory_space=pltpu.HBM)] * 7,
        out_specs=(pl.BlockSpec(memory_space=pltpu.VMEM),) * 5,
        scratch_shapes=[
            *[pltpu.VMEM((rows, chans), bf16)] * 4,
            pltpu.VMEM((ORDER, chans), f32),
            pltpu.VMEM((ORDER, chans), f32),
            pltpu.VMEM((1, chans), f32),
            *[table] * 6,
            pltpu.VMEM((OWNERS * BACK, LANES), f32),
            pltpu.VMEM((cts * (SEG + 1) * ORDER, LANES), f32),
            pltpu.VMEM((cts * (SEG + 1) * ROWS, LANES), f32),
            *[table] * 4,
            pltpu.VMEM((OWNERS * POST, LANES), bf16),
            pltpu.VMEM((CTX * POST, LANES), bf16),
            pltpu.VMEM((CTX * BACK, LANES), bf16),
            pltpu.VMEM((OWNERS * BACK, LANES), bf16),
            pltpu.VMEM((ORDER, LANES), f32),
            pltpu.VMEM((OWNERS * ORDER, LANES), f32),
            pltpu.VMEM((ORDER, LANES), f32),
            pltpu.VMEM((2 * n_tp * PLANES, 1, LANES), f32),
            pltpu.VMEM((1, LANES), f32),
            pltpu.SemaphoreType.DMA((CHUNKS + 3,)),
            pltpu.SemaphoreType.DMA((6,)),
            pltpu.SemaphoreType.DMA((6,)),
        ],
        compiler_params=pltpu.CompilerParams(collective_id=0, has_side_effects=True, vmem_limit_bytes=16 * 2**20),
        name="modal_conv",
    )(
        *[
            pltpu.with_memory_space_constraint(x, pltpu.HBM)
            for x in (queries, keys_in, values_in, cotangent, decay_rates.T, residues.T, skip_gain.reshape(1, chans))
        ]
    )
    outs = pl.pallas_call(
        write,
        out_shape=tuple(jax.ShapeDtypeStruct(o.shape, o.dtype) for o in outs),
        in_specs=[anywhere] * 5,
        out_specs=(pl.BlockSpec(memory_space=pltpu.HBM),) * 5,
        scratch_shapes=[pltpu.SemaphoreType.DMA((5,))],
        name="write_out",
        compiler_params=pltpu.CompilerParams(vmem_limit_bytes=4 * 2**20),
    )(*[pltpu.with_memory_space_constraint(x, pltpu.VMEM) for x in outs])
    return (*outs[:4], outs[4].T)


def solution(mesh):
    line, modes = P("ctx", "tp"), P("tp", None)
    in_specs = (line, line, line, modes, modes, P("tp"), line)
    out_specs = (line, line, line, line, modes)
    return jax.shard_map(shards, mesh=mesh, in_specs=in_specs, out_specs=out_specs, check_vma=False)
```
